128 devices in a mesh: dp: 16 (over y_hi, z, core), head: 8 (over y_lo, x).
Axes of the slice: x: 4, y: 4 (y_hi: 2, y_lo: 2; y = y_hi * 2 + y_lo), z: 4, core: 2. Of those that a mesh axis runs over, the one named last changes fastest.
Arguments:
- projections: bfloat16 [3, 16384, 3072], P(None, ('dp', 'head')), may hold values from -16 to 16
- projection_tangent: bfloat16 [3, 16384, 3072], P(None, ('dp', 'head')), may hold values from -6 to 6
- position_ids: int32 [16384, 3], P(('dp', 'head')), may hold values from 0 to 63
- norm_gain: float32 [2, 3072], replicated, may hold values from 0.5 to 1.5
- out_weight: bfloat16 [3072, 5120], P('dp', 'head'), may hold values from -0.109375 to 0.109375
- timestep: int32 [16], replicated, may hold values from 0 to 999
- time_tangent: float32 [16], replicated, may hold values from 0.5 to 2
- gate_weight: bfloat16 [256, 5120], P('dp'), may hold values from -0.375 to 0.375
- residual: bfloat16 [16384, 5120], P('dp', 'head'), may hold values from -6 to 6
- residual_tangent: bfloat16 [16384, 5120], P('dp', 'head'), may hold values from -6 to 6
Outputs:
- block_out: bfloat16 [16384, 5120], P('dp', 'head')
- block_tangent: bfloat16 [16384, 5120], P('dp', 'head')
The draws below stay inside these ranges and needn't reach their ends.
All inputs are finite; a program needn't handle non-finite values.
Results may differ from the reference program's by a relative error of at most 0.0085.
Values may be sent and summed in bfloat16 or wider, within the bound.
A program may use at most 128 MiB of HBM per device.

```python
import jax
import jax.numpy as jnp
import numpy as np
from jax import lax

D = 5120
HEAD_DIM = 128
FREQ = 256
ATT_W = 3072
SEQ = 1024
CLIPS = 16
TOKENS = 16384
N_HEAD = 8


def draw_projections(key, part):
    key = jax.random.fold_in(key, 7)
    base_key = jax.random.fold_in(key, 0)
    full_shape = (3, TOKENS, ATT_W)
    entries = jax.random.truncated_normal(base_key, -6.0, 6.0, full_shape, jnp.float32)
    return entries.astype(jnp.bfloat16)


def place_ends(result, stream_key, smallest, largest):
    longest = result.shape.index(max(result.shape))
    spots = []
    for shift in (0, 1):
        where = [jax.random.randint(jax.random.fold_in(stream_key, axis), (), 0, length) for axis, length in enumerate(result.shape)]
        where[longest] = (where[longest] + shift) % result.shape[longest]
        spots.append(tuple(where))
    return result.at[spots[0]].set(smallest).at[spots[1]].set(largest)


def levels(own_key, dims, shards, low, high):
    gain = 1.0
    for dim, parts in shards:
        heights = jax.random.uniform(jax.random.fold_in(jax.random.fold_in(own_key, 6), dim), (parts,), jnp.float32, low / len(shards), high / len(shards))
        gain = gain * jnp.repeat(jnp.exp(heights), dims[dim] // parts).reshape((-1,) + (1,) * (len(dims) - 1 - dim))
    return gain


def centred(stream_key, extent, deviation, reach, shards=(), kind=jnp.bfloat16):
    gain = levels(stream_key, extent, shards, -0.22, 0.18) if shards else 1.0
    result = jax.random.normal(stream_key, extent, jnp.float32) * deviation * gain
    return jnp.minimum(jnp.maximum(result, -reach), reach).astype(kind)


def setup_inputs(seed: int = 0) -> dict:
    arg_keys = jax.random.split(jax.random.key(seed), 11)
    projections = draw_projections(jax.random.fold_in(arg_keys[10], 71), 0)
    projection_tangent = centred(arg_keys[1], (3, TOKENS, ATT_W), 1.0, 6.0, ((1, 128),))
    position_ids = place_ends(jax.random.randint(arg_keys[2], (TOKENS, 3), 0, 64), jax.random.fold_in(arg_keys[2], 1), 0, 63).astype(jnp.int32)
    norm_gain = jnp.clip(1.0 + 0.1 * jax.random.normal(arg_keys[3], (2, ATT_W), jnp.float32), 0.5, 1.5)
    out_weight = centred(arg_keys[4], (ATT_W, D), ATT_W ** -0.5, 0.109375, ((0, 16), (1, 8)))
    timestep = place_ends(jax.random.randint(arg_keys[5], (CLIPS,), 0, 1000), jax.random.fold_in(arg_keys[5], 1), 0, 999).astype(jnp.int32)
    time_tangent = jnp.clip(jax.random.uniform(arg_keys[6], (CLIPS,), jnp.float32, 0.5, 2.0), 0.5, 2.0)
    gate_weight = centred(arg_keys[7], (FREQ, D), FREQ ** -0.5, 0.375, ((0, 16),))
    residual = centred(arg_keys[8], (TOKENS, D), 1.0, 6.0, ((0, 16), (1, 8)))
    residual_tangent = centred(arg_keys[9], (TOKENS, D), 1.0, 6.0, ((0, 16), (1, 8)))
    return {"projections": projections, "projection_tangent": projection_tangent, "position_ids": position_ids, "norm_gain": norm_gain, "out_weight": out_weight, "timestep": timestep, "time_tangent": time_tangent, "gate_weight": gate_weight, "residual": residual, "residual_tangent": residual_tangent}


EPSILON = 1e-06

def rope_angles(position_ids):
    pair_count = HEAD_DIM // 2
    height_pairs = HEAD_DIM // 6
    time_pairs = pair_count - 2 * height_pairs
    pair_index = np.arange(pair_count)
    axis_pick = np.where(pair_index < time_pairs, 0, np.where(pair_index < time_pairs + height_pairs, 1, 2))
    local_idx = np.where(axis_pick == 0, pair_index, np.where(axis_pick == 1, pair_index - time_pairs, pair_index - time_pairs - height_pairs))
    span_count = np.where(axis_pick == 0, time_pairs, height_pairs)
    frequency = np.power(10000.0, -local_idx / span_count).astype(np.float32)
    chosen = position_ids.astype(jnp.float32)[:, axis_pick]
    angles = jnp.repeat(chosen * jnp.asarray(frequency), 2, axis=1)
    return (jnp.cos(angles), jnp.sin(angles))

def rotate(matrix, cosine, sine_part):
    row_count = matrix.shape[0]
    heads_here = matrix.shape[1] // HEAD_DIM
    pairs_view = matrix.reshape(row_count, heads_here, HEAD_DIM // 2, 2)
    swapped = jnp.stack([-pairs_view[..., 1], pairs_view[..., 0]], axis=-1).reshape(row_count, heads_here, HEAD_DIM)
    grouped = matrix.reshape(row_count, heads_here, HEAD_DIM)
    turned = grouped * cosine[:, None, :] + swapped * sine_part[:, None, :]
    return turned.reshape(row_count, heads_here * HEAD_DIM)

def norm_tangent(primal, tangent, gains):
    primal_f = primal.astype(jnp.float32)
    tangent_f = tangent.astype(jnp.float32)
    inverse = lax.rsqrt(lax.optimization_barrier(jnp.mean(primal_f * primal_f, axis=1, keepdims=True)) + EPSILON)
    cross = lax.optimization_barrier(jnp.mean(primal_f * tangent_f, axis=1, keepdims=True))
    normed = primal_f * inverse * gains
    normed_tan = gains * (tangent_f * inverse - primal_f * inverse * inverse * inverse * cross)
    return (normed, normed_tan)

def prepare(proj_rows, tangent_rows, position_ids, norm_gain):
    cosine, sine_part = rope_angles(position_ids)
    query_n, query_dn = norm_tangent(proj_rows[0], tangent_rows[0], norm_gain[0])
    key_n, key_dn = norm_tangent(proj_rows[1], tangent_rows[1], norm_gain[1])
    queries = rotate(query_n, cosine, sine_part).astype(jnp.bfloat16)
    key_rows = rotate(key_n, cosine, sine_part).astype(jnp.bfloat16)
    query_tan = rotate(query_dn, cosine, sine_part).astype(jnp.bfloat16)
    key_tan = rotate(key_dn, cosine, sine_part).astype(jnp.bfloat16)
    return (queries, key_rows, proj_rows[2], query_tan, key_tan, tangent_rows[2])

def transposed_dot(left_side, right_side):
    return lax.dot_general(left_side, right_side, (((1,), (1,)), ((), ())), preferred_element_type=jnp.float32)

def attend_head(queries, key_rows, val_rows, query_tan, key_tan, val_tan):
    length = queries.shape[0]
    block_rows = min(512, length)
    blocks = length // block_rows
    factor = HEAD_DIM ** (-0.5)

    def one_block(inputs):
        query_block, query_tan_block = inputs
        scores = transposed_dot(query_block, key_rows) * factor
        shifted = scores - lax.optimization_barrier(jnp.max(scores, axis=1, keepdims=True))
        weights = jnp.exp(shifted)
        probability = weights / lax.optimization_barrier(jnp.sum(weights, axis=1, keepdims=True))
        prob_low = probability.astype(jnp.bfloat16)
        output = jnp.dot(prob_low, val_rows, preferred_element_type=jnp.float32)
        score_tan = (transposed_dot(query_tan_block, key_rows) + transposed_dot(query_block, key_tan)) * factor
        weighted = probability * score_tan
        prob_tan = (weighted - probability * lax.optimization_barrier(jnp.sum(weighted, axis=1, keepdims=True))).astype(jnp.bfloat16)
        output_tan = jnp.dot(prob_tan, val_rows, preferred_element_type=jnp.float32) + jnp.dot(prob_low, val_tan, preferred_element_type=jnp.float32)
        return (output.astype(jnp.bfloat16), output_tan.astype(jnp.bfloat16))
    width = queries.shape[1]
    results = lax.map(one_block, (queries.reshape(blocks, block_rows, width), query_tan.reshape(blocks, block_rows, width)))
    return (results[0].reshape(length, width), results[1].reshape(length, width))

def attend_heads(queries, key_rows, val_rows, query_tan, key_tan, val_tan):
    length = queries.shape[0]
    heads_here = queries.shape[1] // HEAD_DIM

    def split_heads(matrix):
        return matrix.reshape(matrix.shape[0], heads_here, HEAD_DIM).transpose(1, 0, 2)

    def one_head(inputs):
        return attend_head(*inputs)
    stacked = tuple((split_heads(matrix) for matrix in (queries, key_rows, val_rows, query_tan, key_tan, val_tan)))
    outputs, outputs_tan = lax.map(one_head, stacked)
    return (outputs.transpose(1, 0, 2).reshape(length, heads_here * HEAD_DIM), outputs_tan.transpose(1, 0, 2).reshape(length, heads_here * HEAD_DIM))

def embed_time(timestep, time_tangent):
    half_freq = FREQ // 2
    frequency = jnp.power(10000.0, -jnp.arange(half_freq, dtype=jnp.float32) / half_freq)
    angles = timestep.astype(jnp.float32)[:, None] * frequency[None, :]
    embedding = jnp.concatenate([jnp.cos(angles), jnp.sin(angles)], axis=1)
    embed_tan = jnp.concatenate([-frequency * jnp.sin(angles), frequency * jnp.cos(angles)], axis=1) * time_tangent[:, None]
    return (embedding.astype(jnp.bfloat16), embed_tan.astype(jnp.bfloat16))

def project_groups(outputs, weight):
    length = outputs.shape[0]
    group_width = outputs.shape[1] // N_HEAD
    grouped = outputs.reshape(length, N_HEAD, group_width).transpose(1, 0, 2)
    weight_groups = weight.reshape(N_HEAD, group_width, weight.shape[1])

    def add_group(total, inputs):
        part_out, part_weight = inputs
        term = jnp.dot(part_out, part_weight, preferred_element_type=jnp.float32).astype(jnp.bfloat16)
        term = lax.optimization_barrier(term)
        return (total + term.astype(jnp.float32), None)
    start_total = jnp.zeros((length, weight.shape[1]), jnp.float32)
    total, unused = lax.scan(add_group, start_total, (grouped, weight_groups))
    return total

def reference(projections, projection_tangent, position_ids, norm_gain, out_weight, timestep, time_tangent, gate_weight, residual, residual_tangent):
    embedding, embed_tan = embed_time(timestep, time_tangent)
    gates = jnp.dot(embedding, gate_weight, preferred_element_type=jnp.float32)
    gates_tan = jnp.dot(embed_tan, gate_weight, preferred_element_type=jnp.float32)
    clip_proj = projections.reshape(3, CLIPS, SEQ, ATT_W).transpose(1, 0, 2, 3)
    clip_tan = projection_tangent.reshape(3, CLIPS, SEQ, ATT_W).transpose(1, 0, 2, 3)
    clip_pos = position_ids.reshape(CLIPS, SEQ, 3)
    clip_res = residual.reshape(CLIPS, SEQ, D)
    clip_res_tan = residual_tangent.reshape(CLIPS, SEQ, D)

    def one_clip(inputs):
        proj_rows, tangent_rows, pos_rows, gate_vec, gate_tan, res_rows, res_tan = inputs
        prepared = prepare(proj_rows, tangent_rows, pos_rows, norm_gain)
        outputs, outputs_tan = attend_heads(*prepared)
        attended = project_groups(outputs, out_weight)
        attended_tan = project_groups(outputs_tan, out_weight)
        mixed_out = (res_rows.astype(jnp.float32) + gate_vec[None, :] * attended).astype(jnp.bfloat16)
        mixed_tan = (res_tan.astype(jnp.float32) + gate_tan[None, :] * attended + gate_vec[None, :] * attended_tan).astype(jnp.bfloat16)
        return (mixed_out, mixed_tan)
    block_out, block_tangent = lax.map(one_clip, (clip_proj, clip_tan, clip_pos, gates, gates_tan, clip_res, clip_res_tan))
    return (block_out.reshape(TOKENS, D), block_tangent.reshape(TOKENS, D))
```

```python
import math

import jax
import jax.numpy as jnp
import numpy as np
from jax import lax
from jax.experimental import pallas as pl
from jax.experimental.pallas import tpu as pltpu
from jax.sharding import PartitionSpec as P

HEAD_DIM = 128
ATT_W = 3072
EPSILON = 1e-06
MESH = pl.DeviceIdType.MESH
BF = jnp.bfloat16
F32 = jnp.float32

X = 4
ROWS = 128
SEQ = 1024
HALF = 512
GW = 384
COLS = 640
FACTOR = HEAD_DIM ** (-0.5)

ORDER = ((1, 0), (0, 1), (0, 3), (1, 2), (0, 2), (1, 1), (1, 3))


def constants():
    pair_count = HEAD_DIM // 2
    height_pairs = HEAD_DIM // 6
    time_pairs = pair_count - 2 * height_pairs
    j = np.arange(pair_count)
    local = np.where(
        j < time_pairs,
        j,
        np.where(j < time_pairs + height_pairs, j - time_pairs, j - time_pairs - height_pairs),
    )
    span = np.where(j < time_pairs, time_pairs, height_pairs)
    rope = np.repeat(np.power(10000.0, -local / span), 2)
    clock = np.power(10000.0, -np.arange(128) / 128)
    rows = np.zeros((8, 128), np.float32)
    rows[0] = rope
    rows[1] = clock
    return rows, 2 * time_pairs, 2 * (time_pairs + height_pairs)


CONST, LANE_ROW, LANE_COL = constants()


def nt_dot(a, b):
    return lax.dot_general(a, b, (((1,), (1,)), ((), ())), preferred_element_type=F32)


def kernel(
    proj,
    tan,
    pos,
    gain,
    wout,
    time,
    ttan,
    wgate,
    res,
    rtan,
    const,
    out,
    otan,
    raw,
    sv,
    sq,
    recv,
    ob,
    pb,
    wall,
    gall,
    resv,
    po,
    pr,
    load_sem,
    res_sem,
    v_send,
    v_recv,
    q_send,
    q_recv,
    pre_send,
    pre_recv,
    w_send,
    w_recv,
    g_send,
    g_recv,
    x_send,
    x_recv,
    y_send,
    y_recv,
):
    dp = lax.axis_index("dp")
    head = lax.axis_index("head")
    y, x = head // X, lax.rem(head, X)
    yh, z, c = dp // 8, lax.rem(dp // 2, 4), lax.rem(dp, 2)
    partner = {"dp": dp, "head": (1 - y) * X + x}
    right = {"dp": dp, "head": y * X + lax.rem(x + 1, X)}
    left = {"dp": dp, "head": y * X + lax.rem(x + 3, X)}
    xl, xr = lax.rem(x + 3, X), lax.rem(x + 1, X)
    other_core = {"dp": dp + 1 - 2 * c, "head": head}

    def z_peer(d):
        return {"dp": yh * 8 + lax.rem(z + d, 4) * 2 + c, "head": head}

    def y_peer(yl):
        return {"dp": (1 - yh) * 8 + z * 2 + c, "head": yl * X + x}

    def send(src, dst, ssem, rsem, to):
        pltpu.make_async_remote_copy(
            src_ref=src,
            dst_ref=dst,
            send_sem=ssem,
            recv_sem=rsem,
            device_id=to,
            device_id_type=MESH,
        ).start()

    def local(src, dst, sem):
        pltpu.make_async_copy(src, dst, sem).start()

    def wait(ref, sem):
        pltpu.make_async_copy(ref, ref, sem).wait()

    for h in range(3):

        def load_v(g, _, h=h):
            col = pl.ds(pl.multiple_of(g * GW + h * 128, 128), 128)
            local(proj.at[2, :, col], sv.at[h, g, :, pl.ds(0, 128)], load_sem.at[h])
            local(tan.at[2, :, col], sv.at[h, g, :, pl.ds(128, 128)], load_sem.at[h])
            return 0

        lax.fori_loop(0, 8, load_v, 0)
    local(proj.at[pl.ds(0, 2)], raw.at[0], load_sem.at[3])
    local(tan.at[pl.ds(0, 2)], raw.at[1], load_sem.at[3])
    local(wout, wall.at[y, yh, z, c], w_recv.at[0])
    local(
        wgate.at[:, pl.ds(pl.multiple_of(head * COLS, 128), COLS)],
        gall.at[yh, z, c],
        g_recv.at[0],
    )
    local(res, resv.at[0], res_sem)
    local(rtan, resv.at[1], res_sem)

    barrier = pltpu.get_barrier_semaphore()
    for dy, dx in ORDER:
        to = {"dp": dp, "head": lax.rem(y + dy, 2) * X + lax.rem(x + dx, X)}
        pl.semaphore_signal(barrier, inc=1, device_id=to, device_id_type=MESH)
    for d in (1, 2, 3):
        pl.semaphore_signal(barrier, inc=1, device_id=z_peer(d), device_id_type=MESH)
    pl.semaphore_signal(barrier, inc=1, device_id=other_core, device_id_type=MESH)
    for yl in (0, 1):
        pl.semaphore_signal(barrier, inc=1, device_id=y_peer(yl), device_id_type=MESH)
    pl.semaphore_wait(barrier, 13)

    for to in (partner, y_peer(0), y_peer(1)):
        send(wout, wall.at[y, yh, z, c], w_send.at[0], w_recv.at[0], to)
    mine = pl.ds(pl.multiple_of(head * ROWS, ROWS), ROWS)
    for h in range(3):
        wait(sv.at[h], load_sem.at[h])
        for dy, dx in ORDER:
            ty, tx = lax.rem(y + dy, 2), lax.rem(x + dx, X)
            g = ty * X + tx
            send(
                sv.at[h, g],
                recv.at[h, 2, mine],
                v_send.at[h],
                v_recv.at[h],
                {"dp": dp, "head": g},
            )
        local(sv.at[h, head], recv.at[h, 2, mine], v_recv.at[h])
    send(
        wgate.at[:, pl.ds(pl.multiple_of(head * COLS, 128), COLS)],
        gall.at[yh, z, c],
        g_send.at[0],
        g_recv.at[0],
        {"dp": (1 - yh) * 8 + z * 2 + c, "head": head},
    )

    lane = lax.broadcasted_iota(jnp.int32, (ROWS, 128), 1)
    ids = pos[...].astype(F32)
    chosen = jnp.where(
        lane < LANE_ROW, ids[:, 0:1], jnp.where(lane < LANE_COL, ids[:, 1:2], ids[:, 2:3])
    )
    angle = chosen * const[0:1, :]
    cosine = jnp.cos(angle)
    even = lax.rem(lane, 2) == 0
    sine = jnp.where(even, -jnp.sin(angle), jnp.sin(angle))

    def rotate(m):
        swapped = jnp.where(even, pltpu.roll(m, 127, 1), pltpu.roll(m, 1, 1))
        return (m * cosine + swapped * sine).astype(BF)

    wait(raw, load_sem.at[3])
    stats = []
    for a in (0, 1):

        def add(i, carry, a=a):
            square, cross = carry
            col = pl.ds(pl.multiple_of(i * 128, 128), 128)
            q = raw[0, a, :, col].astype(F32)
            dq = raw[1, a, :, col].astype(F32)
            return square + q * q, cross + q * dq

        zero = jnp.zeros((ROWS, 128), F32)
        square, cross = lax.fori_loop(0, ATT_W // 128, add, (zero, zero))
        r = lax.rsqrt(jnp.sum(square, axis=1, keepdims=True) / ATT_W + EPSILON)
        cr = jnp.sum(cross, axis=1, keepdims=True) / ATT_W
        stats.append((r, r * r * r * cr))

    for h in range(3):

        def prepare(i, _, h=h):
            ty, tx = lax.rem(y + i // X, 2), lax.rem(x + i, X)
            g = ty * X + tx
            col = pl.ds(pl.multiple_of(g * GW + h * 128, 128), 128)
            for a in (0, 1):
                r, rc = stats[a]
                q = raw[0, a, :, col].astype(F32)
                dq = raw[1, a, :, col].astype(F32)
                gn = gain[a : a + 1, col]
                n = rotate(q * r * gn)
                dn = rotate(gn * (dq * r - q * rc))
                if a == 0:
                    sq[h, g, 0, :, 0:128] = dn
                    sq[h, g, 0, :, 128:256] = n
                else:
                    sq[h, g, 1, :, 0:128] = n
                    sq[h, g, 1, :, 128:256] = dn

            @pl.when(i > 0)
            def _():
                send(
                    sq.at[h, g],
                    recv.at[h, pl.ds(0, 2), mine],
                    q_send.at[h],
                    q_recv.at[h],
                    {"dp": dp, "head": g},
                )

            return 0

        lax.fori_loop(0, 8, prepare, 0)
        local(sq.at[h, head], recv.at[h, pl.ds(0, 2), mine], q_recv.at[h])

    wait(wall.at[:, :, z, c], w_recv.at[0])
    wait(gall.at[:, z, c], g_recv.at[0])
    for d in (1, 3, 2):
        send(wall.at[:, :, z, c], wall.at[:, :, z, c], w_send.at[1], w_recv.at[1], z_peer(d))
        send(gall.at[:, z, c], gall.at[:, z, c], g_send.at[1], g_recv.at[1], z_peer(d))

    def attend(h, block):
        rows = pl.ds(pl.multiple_of(block * 256, 256), 256)
        qd = recv[h, 0, rows, :]
        kd = recv[h, 1]
        s = nt_dot(qd[:, 128:], kd[:, :128])
        ds = nt_dot(qd, kd)
        top = jnp.max(s, axis=1, keepdims=True)
        e = jnp.exp2((s - top) * (FACTOR * math.log2(math.e)))
        inv = 1.0 / jnp.sum(e, axis=1, keepdims=True)
        mu = jnp.sum(e * ds, axis=1, keepdims=True) * inv
        t = (e * (ds - mu)).astype(BF)
        vd = recv[h, 2]
        both = jnp.dot(e.astype(BF), vd, preferred_element_type=F32)
        turn = jnp.dot(t, vd[:, :128], preferred_element_type=F32)
        o = both[:, :128] * inv
        do = (both[:, 128:] + turn * FACTOR) * inv
        return o.astype(BF), do.astype(BF)

    def x_unit(rb, part):
        width = 256 if part == 0 else 128
        col = pl.ds(pl.multiple_of(x * GW + part * 256, 128), width)
        k = rb * 2 + part
        src = ob.at[rb, :, :, :, col]
        send(src, src, x_send.at[0], x_recv.at[0, k], right)
        send(src, src, x_send.at[1], x_recv.at[1, k], left)

    def forward(rb, part):
        width = 256 if part == 0 else 128
        k = rb * 2 + part
        col = pl.ds(pl.multiple_of(xl * GW + part * 256, 128), width)
        wait(ob.at[rb, :, :, :, col], x_recv.at[0, k])
        src = ob.at[rb, :, 0, :, col]
        send(src, src, x_send.at[2], x_recv.at[2, k], right)
        col = pl.ds(pl.multiple_of(xr * GW + part * 256, 128), width)
        wait(ob.at[rb, :, :, :, col], x_recv.at[1, k])
        src = ob.at[rb, :, 1, :, col]
        send(src, src, x_send.at[3], x_recv.at[3, k], left)

    for h in range(3):
        wait(recv.at[h, 2], v_recv.at[h])
        wait(recv.at[h, pl.ds(0, 2)], q_recv.at[h])
        own_col = pl.ds(pl.multiple_of(x * GW + h * 128, 128), 128)

        def for_partner(j, _, h=h):
            o, do = attend(h, (1 - y) * 2 + j)
            for i in (0, 1):
                pb[h, j * 2 + i, 0] = o[i * 128 : (i + 1) * 128]
                pb[h, j * 2 + i, 1] = do[i * 128 : (i + 1) * 128]
            return 0

        def for_self(j, _, h=h):
            o, do = attend(h, y * 2 + j)
            for i in (0, 1):
                ob[j * 2 + i, y, 0, :, own_col] = o[i * 128 : (i + 1) * 128]
                ob[j * 2 + i, y, 1, :, own_col] = do[i * 128 : (i + 1) * 128]
            return 0

        if h == 2:
            wait(ob.at[:, 0, :, :, pl.ds(0, 128)], pre_recv.at[0])
            wait(ob.at[:, 0, :, :, pl.ds(0, 128)], pre_recv.at[1])
            for rb in (0, 1):
                x_unit(rb, 0)
        lax.fori_loop(0, 2, for_partner, 0)
        send(pb.at[h], ob.at[:, y, :, :, own_col], pre_send.at[h], pre_recv.at[h], partner)
        lax.fori_loop(0, 2, for_self, 0)

    wait(wall.at[:, :, pl.ds(0, 3), c], w_recv.at[1])
    wait(gall.at[:, pl.ds(0, 3), c], g_recv.at[1])
    send(wall.at[:, :, :, c], wall.at[:, :, :, c], w_send.at[2], w_recv.at[2], other_core)
    send(gall.at[:, :, c], gall.at[:, :, c], g_send.at[2], g_recv.at[2], other_core)

    wait(ob.at[:, 0, :, :, pl.ds(0, 128)], pre_recv.at[2])
    x_unit(0, 1)
    x_unit(1, 1)
    for rb in (2, 3):
        x_unit(rb, 0)
        x_unit(rb, 1)

    wait(wall.at[:, :, :, 1 - c], w_recv.at[2])
    wait(gall.at[:, :, 1 - c], g_recv.at[2])
    moment = time[dp].astype(F32)
    speed = ttan[dp]
    freq = const[1:2, :]
    cos_t, sin_t = jnp.cos(moment * freq), jnp.sin(moment * freq)
    row = lax.broadcasted_iota(jnp.int32, (16, 256), 0)
    emb = jnp.concatenate([cos_t, sin_t], axis=1)
    demb = jnp.concatenate([-freq * sin_t, freq * cos_t], axis=1) * speed
    embs = jnp.where(row == 0, emb, jnp.where(row == 1, demb, 0.0)).astype(BF)
    gates = jnp.dot(embs, gall[...].reshape(256, COLS), preferred_element_type=F32)
    gate, dgate = gates[0:1], gates[1:2]

    wait(resv, res_sem)

    def finish(rows, attn, dattn):
        out[rows, :] = (resv[0, rows, :].astype(F32) + gate * attn).astype(BF)
        otan[rows, :] = (resv[1, rows, :].astype(F32) + dgate * attn + gate * dattn).astype(BF)

    def project(rb, yl):
        total = None
        for gy in (0, 1):
            term = jnp.dot(
                ob[rb, gy].reshape(256, 1536),
                wall[yl, gy].reshape(1536, COLS),
                preferred_element_type=F32,
            )
            total = term if total is None else total + term
        return total

    def forwards(rb, _):
        for part, width in ((0, 256), (1, 128)):
            k = rb * 2 + part
            col = pl.ds(pl.multiple_of(xl * GW + part * 256, 128), width)
            wait(ob.at[rb, :, :, :, col], x_recv.at[0, k])
            src = ob.at[rb, :, 0, :, col]
            send(src, src, x_send.at[2], x_recv.at[2, k], right)
            col = pl.ds(pl.multiple_of(xr * GW + part * 256, 128), width)
            wait(ob.at[rb, :, :, :, col], x_recv.at[1, k])
            src = ob.at[rb, :, 1, :, col]
            send(src, src, x_send.at[3], x_recv.at[3, k], left)
        return 0

    forwards(0, 0)

    def row_block(rb, _):
        @pl.when(rb < 3)
        def _():
            forwards(rb + 1, 0)

        for part, width in ((0, 256), (1, 128)):
            k = rb * 2 + part
            wait(ob.at[rb, :, 0, :, pl.ds(0, width)], x_recv.at[2, k])
            wait(ob.at[rb, :, 1, :, pl.ds(0, width)], x_recv.at[3, k])
        total = project(rb, 1 - y)
        po[rb] = total.astype(BF)
        send(po.at[rb], pr.at[rb], y_send.at[rb], y_recv.at[rb], partner)
        total = project(rb, y)
        rows = pl.ds(pl.multiple_of(y * HALF + rb * 128, 128), 128)
        finish(rows, total[:128], total[128:])
        return 0

    lax.fori_loop(0, 4, row_block, 0)

    def partner_block(rb, _):
        wait(pr.at[rb], y_recv.at[rb])
        rows = pl.ds(pl.multiple_of((1 - y) * HALF + rb * 128, 128), 128)
        finish(rows, pr[rb, 0:128].astype(F32), pr[rb, 128:256].astype(F32))
        return 0

    lax.fori_loop(0, 4, partner_block, 0)

    for h in range(3):
        wait(sv.at[h, pl.ds(0, 7)], v_send.at[h])
        wait(sq.at[h, pl.ds(0, 7)], q_send.at[h])
        wait(pb.at[h], pre_send.at[h])
    wait(wall.at[0, 0, pl.ds(0, 3), 0], w_send.at[0])
    wait(wall.at[:, :, pl.ds(0, 3), 0], w_send.at[1])
    wait(wall.at[:, :, :, 0], w_send.at[2])
    wait(gall.at[0, 0, 0], g_send.at[0])
    wait(gall.at[:, pl.ds(0, 3), 0], g_send.at[1])
    wait(gall.at[:, :, 0], g_send.at[2])
    wait(ob.at[:, :, :, :, pl.ds(0, GW)], x_send.at[0])
    wait(ob.at[:, :, :, :, pl.ds(0, GW)], x_send.at[1])
    wait(ob.at[:, :, 0, :, pl.ds(0, GW)], x_send.at[2])
    wait(ob.at[:, :, 1, :, pl.ds(0, GW)], x_send.at[3])
    for rb in range(4):
        wait(po.at[rb], y_send.at[rb])


def per_device(
    projections,
    projection_tangent,
    position_ids,
    norm_gain,
    out_weight,
    timestep,
    time_tangent,
    gate_weight,
    residual,
    residual_tangent,
):
    anywhere = pl.BlockSpec(memory_space=pl.ANY)
    vmem = pl.BlockSpec(memory_space=pltpu.VMEM)
    smem = pl.BlockSpec(memory_space=pltpu.SMEM)
    dma = pltpu.SemaphoreType.DMA
    shape = jax.ShapeDtypeStruct((SEQ, COLS), BF)
    return pl.pallas_call(
        kernel,
        out_shape=(shape, shape),
        in_specs=[
            anywhere,
            anywhere,
            vmem,
            vmem,
            anywhere,
            smem,
            smem,
            anywhere,
            anywhere,
            anywhere,
            vmem,
        ],
        out_specs=(vmem, vmem),
        scratch_shapes=[
            pltpu.VMEM((2, 2, ROWS, ATT_W), BF),
            pltpu.VMEM((3, 8, ROWS, 256), BF),
            pltpu.VMEM((3, 8, 2, ROWS, 256), BF),
            pltpu.VMEM((3, 3, SEQ, 256), BF),
            pltpu.VMEM((4, 2, 2, ROWS, 1536), BF),
            pltpu.VMEM((3, 4, 2, ROWS, 128), BF),
            pltpu.VMEM((2, 2, 4, 2, 192, COLS), BF),
            pltpu.VMEM((2, 4, 2, 16, COLS), BF),
            pltpu.VMEM((2, SEQ, COLS), BF),
            pltpu.VMEM((4, 256, COLS), BF),
            pltpu.VMEM((4, 256, COLS), BF),
            dma((4,)),
            dma,
            dma((3,)),
            dma((3,)),
            dma((3,)),
            dma((3,)),
            dma((3,)),
            dma((3,)),
            dma((3,)),
            dma((3,)),
            dma((3,)),
            dma((3,)),
            dma((4,)),
            dma((4, 8)),
            dma((4,)),
            dma((4,)),
        ],
        compiler_params=pltpu.CompilerParams(
            collective_id=0, has_side_effects=True, vmem_limit_bytes=60 * 2**20
        ),
    )(
        projections,
        projection_tangent,
        position_ids,
        norm_gain,
        out_weight,
        timestep,
        time_tangent,
        gate_weight,
        residual,
        residual_tangent,
        jnp.asarray(CONST),
    )


def solution(mesh):
    placed = (
        P(None, ("dp", "head"), None),
        P(None, ("dp", "head"), None),
        P(("dp", "head"), None),
        P(),
        P("dp", "head"),
        P(),
        P(),
        P("dp", None),
        P("dp", "head"),
        P("dp", "head"),
    )
    return jax.shard_map(
        per_device,
        mesh=mesh,
        in_specs=placed,
        out_specs=(P("dp", "head"), P("dp", "head")),
        check_vma=False,
    )
```

```python
import math

import jax
import jax.numpy as jnp
import numpy as np
from jax import lax
from jax.experimental import pallas as pl
from jax.experimental.pallas import tpu as pltpu
from jax.sharding import PartitionSpec as P

HEAD_DIM = 128
ATT_W = 3072
EPSILON = 1e-06
MESH = pl.DeviceIdType.MESH
BF = jnp.bfloat16
F32 = jnp.float32

X = 4
ROWS = 128
SEQ = 1024
HALF = 512
GW = 384
COLS = 640
FACTOR = HEAD_DIM ** (-0.5)

PIECES = ((0, 0, 128), (1, 0, 128), (2, 0, 128), (3, 0, 64), (3, 64, 64))
PARTS = ((0, 256), (256, 128), (0, 384))

ORDER = ((1, 0), (0, 1), (0, 3), (1, 2), (0, 2), (1, 1), (1, 3))


def constants():
    pair_count = HEAD_DIM // 2
    height_pairs = HEAD_DIM // 6
    time_pairs = pair_count - 2 * height_pairs
    j = np.arange(pair_count)
    local = np.where(
        j < time_pairs,
        j,
        np.where(j < time_pairs + height_pairs, j - time_pairs, j - time_pairs - height_pairs),
    )
    span = np.where(j < time_pairs, time_pairs, height_pairs)
    rope = np.repeat(np.power(10000.0, -local / span), 2)
    clock = np.power(10000.0, -np.arange(128) / 128)
    rows = np.zeros((8, 128), np.float32)
    rows[0] = rope
    rows[1] = clock
    return rows, 2 * time_pairs, 2 * (time_pairs + height_pairs)


CONST, LANE_ROW, LANE_COL = constants()


def nt_dot(a, b):
    return lax.dot_general(a, b, (((1,), (1,)), ((), ())), preferred_element_type=F32)


def kernel(
    proj,
    tan,
    pos_hbm,
    gain_hbm,
    wout,
    time_hbm,
    ttan_hbm,
    wgate,
    res,
    rtan,
    const_hbm,
    out,
    otan,
    pos,
    gain,
    time,
    ttan,
    const,
    raw,
    sv,
    sq,
    recv,
    ob,
    pb,
    wall,
    gall,
    resv,
    outv,
    po,
    pr,
    small_sem,
    load_sem,
    res_sem,
    out_sem,
    v_send,
    v_recv,
    q_send,
    q_recv,
    pre_send,
    pre_recv,
    wy_send,
    wy_recv,
    wz_send,
    wz_recv,
    wc_send,
    wc_recv,
    g_send,
    g_recv,
    x_send,
    x_recv,
    y_send,
    y_recv,
):
    dp = lax.axis_index("dp")
    head = lax.axis_index("head")
    y, x = head // X, lax.rem(head, X)
    yh, z, c = dp // 8, lax.rem(dp // 2, 4), lax.rem(dp, 2)
    partner = {"dp": dp, "head": (1 - y) * X + x}
    right = {"dp": dp, "head": y * X + lax.rem(x + 1, X)}
    left = {"dp": dp, "head": y * X + lax.rem(x + 3, X)}
    xl, xr = lax.rem(x + 3, X), lax.rem(x + 1, X)
    other_core = {"dp": dp + 1 - 2 * c, "head": head}

    def z_peer(d):
        return {"dp": yh * 8 + lax.rem(z + d, 4) * 2 + c, "head": head}

    def send(src, dst, ssem, rsem, to):
        pltpu.make_async_remote_copy(
            src_ref=src,
            dst_ref=dst,
            send_sem=ssem,
            recv_sem=rsem,
            device_id=to,
            device_id_type=MESH,
        ).start()

    def local(src, dst, sem):
        pltpu.make_async_copy(src, dst, sem).start()

    def wait(ref, sem):
        pltpu.make_async_copy(ref, ref, sem).wait()

    def sends_v(h):
        for dy, dx in ORDER:
            g = lax.rem(y + dy, 2) * X + lax.rem(x + dx, X)
            to = {"dp": dp, "head": g}
            send(sv.at[h, g], recv.at[h, 2, mine], v_send.at[h], v_recv.at[h], to)
        local(sv.at[h, head], recv.at[h, 2, mine], v_recv.at[h])

    def send_q(h, g):
        to = {"dp": dp, "head": g}
        send(sq.at[h, g], recv.at[h, pl.ds(0, 2), mine], q_send.at[h], q_recv.at[h], to)

    def sends_q(h):
        for dy, dx in ORDER:
            send_q(h, lax.rem(y + dy, 2) * X + lax.rem(x + dx, X))
        local(sq.at[h, head], recv.at[h, pl.ds(0, 2), mine], q_recv.at[h])

    def shard(s):
        return wall.at[y if s in (0, 2) else 1 - y, yh if s in (0, 1) else 1 - yh]

    def y_chip(s):
        row = yh if s in (0, 1) else 1 - yh
        return {
            "dp": row * 8 + z * 2 + c,
            "head": (y if s in (0, 2) else 1 - y) * X + x,
        }

    def shard_along_z(s):
        for d in (1, 3, 2):
            src = shard(s).at[z, c]
            send(src, src, wz_send.at[s], wz_recv.at[s], z_peer(d))

    def shard_to_core(s):
        wait(shard(s).at[pl.ds(0, 3), c], wz_recv.at[s])
        src = shard(s).at[:, c]
        send(src, src, wc_send.at[s], wc_recv.at[s], other_core)

    mine = pl.ds(pl.multiple_of(head * ROWS, ROWS), ROWS)
    gate_cols = wgate.at[:, pl.ds(pl.multiple_of(head * COLS, 128), COLS)]

    for h in range(3):

        def load_v(g, _, h=h):
            col = pl.ds(pl.multiple_of(g * GW + h * 128, 128), 128)
            local(proj.at[2, :, col], sv.at[h, g, :, pl.ds(0, 128)], load_sem.at[h])
            local(tan.at[2, :, col], sv.at[h, g, :, pl.ds(128, 128)], load_sem.at[h])
            return 0

        lax.fori_loop(0, 8, load_v, 0)
    local(wout, shard(0).at[z, c], wy_recv.at[0])
    small = ((pos_hbm, pos), (gain_hbm, gain), (time_hbm, time), (ttan_hbm, ttan), (const_hbm, const))
    for i, (src, dst) in enumerate(small):
        local(src, dst, small_sem.at[i])
    local(proj.at[pl.ds(0, 2)], raw.at[0], load_sem.at[3])
    local(tan.at[pl.ds(0, 2)], raw.at[1], load_sem.at[3])
    local(gate_cols, gall.at[yh, z, c], g_recv.at[0])
    local(res, resv.at[0], res_sem)
    local(rtan, resv.at[1], res_sem)

    barrier = pltpu.get_barrier_semaphore()
    for dy, dx in ORDER:
        to = {"dp": dp, "head": lax.rem(y + dy, 2) * X + lax.rem(x + dx, X)}
        pl.semaphore_signal(barrier, inc=1, device_id=to, device_id_type=MESH)
    for to in (z_peer(1), z_peer(2), z_peer(3), other_core, y_chip(2), y_chip(3)):
        pl.semaphore_signal(barrier, inc=1, device_id=to, device_id_type=MESH)
    pl.semaphore_wait(barrier, 13)

    wait(shard(0).at[z, c], wy_recv.at[0])
    src = shard(0).at[z, c]
    send(src, src, wy_send.at[3], wy_recv.at[3], y_chip(3))
    shard_along_z(0)
    for h in (0, 1):
        wait(sv.at[h], load_sem.at[h])
        sends_v(h)
    send(gate_cols, gall.at[yh, z, c], g_send.at[0], g_recv.at[0], y_chip(2))

    for i, (_, dst) in enumerate(small):
        wait(dst, small_sem.at[i])

    line = lax.broadcasted_iota(jnp.int32, (128, ROWS), 0)
    ids = pos[...].astype(F32)
    chosen = jnp.where(
        line < LANE_ROW, ids[0:1, :], jnp.where(line < LANE_COL, ids[1:2, :], ids[2:3, :])
    )
    angle = jnp.transpose(chosen) * const[0:1, :]
    lane = lax.broadcasted_iota(jnp.int32, (ROWS, 128), 1)
    even = lax.rem(lane, 2) == 0
    cosine, sine = jnp.cos(angle), jnp.sin(angle)
    sine = jnp.where(even, -sine, sine)

    def rotate(m):
        swapped = jnp.where(even, pltpu.roll(m, 127, 1), pltpu.roll(m, 1, 1))
        return (m * cosine + swapped * sine).astype(BF)

    wait(raw, load_sem.at[3])
    stats = []
    for a in (0, 1):

        def add(i, carry, a=a):
            square, cross = carry
            col = pl.ds(pl.multiple_of(i * 128, 128), 128)
            q = raw[0, a, :, col].astype(F32)
            dq = raw[1, a, :, col].astype(F32)
            return square + q * q, cross + q * dq

        zero = jnp.zeros((ROWS, 128), F32)
        square, cross = lax.fori_loop(0, ATT_W // 128, add, (zero, zero))
        r = lax.rsqrt(jnp.sum(square, axis=1, keepdims=True) / ATT_W + EPSILON)
        cr = jnp.sum(cross, axis=1, keepdims=True) / ATT_W
        stats.append((r, r * r * r * cr))

    for h in range(3):

        def prepare(i, _, h=h):
            g = lax.rem(y + i // X, 2) * X + lax.rem(x + i, X)
            col = pl.ds(pl.multiple_of(g * GW + h * 128, 128), 128)
            for a in (0, 1):
                r, rc = stats[a]
                q = raw[0, a, :, col].astype(F32)
                dq = raw[1, a, :, col].astype(F32)
                gn = gain[a : a + 1, col]
                n = rotate(q * r * gn)
                dn = rotate(gn * (dq * r - q * rc))
                sq[h, g, a, :, 0:128] = dn if a == 0 else n
                sq[h, g, a, :, 128:256] = n if a == 0 else dn

            if h == 0:

                @pl.when(i > 0)
                def _():
                    send_q(h, g)

            return 0

        lax.fori_loop(0, 8, prepare, 0)
        if h == 0:
            local(sq.at[h, head], recv.at[h, pl.ds(0, 2), mine], q_recv.at[h])

    def attend(h, block):
        rows = pl.ds(pl.multiple_of(block * 256, 256), 256)
        qd = recv[h, 0, rows, :]
        kd = recv[h, 1]
        s = nt_dot(qd[:, 128:], kd[:, :128])
        ds = nt_dot(qd, kd)
        top = jnp.max(s, axis=1, keepdims=True)
        e = jnp.exp2((s - top) * (FACTOR * math.log2(math.e)))
        inv = 1.0 / jnp.sum(e, axis=1, keepdims=True)
        mu = jnp.sum(e * ds, axis=1, keepdims=True) * inv
        t = (e * (ds - mu)).astype(BF)
        vd = recv[h, 2]
        both = jnp.dot(e.astype(BF), vd, preferred_element_type=F32)
        turn = jnp.dot(t, vd[:, :128], preferred_element_type=F32)
        o = both[:, :128] * inv
        do = (both[:, 128:] + turn * FACTOR) * inv
        return o.astype(BF), do.astype(BF)

    def swap(h, pair):
        two = pl.ds(pair * 2, 2)
        col = pl.ds(pl.multiple_of(x * GW + h * 128, 128), 128)
        k = h * 2 + pair
        send(pb.at[h, two], ob.at[two, y, :, :, col], pre_send.at[k], pre_recv.at[k], partner)

    def swapped(h, pair):
        wait(ob.at[pl.ds(pair * 2, 2), 0, :, :, pl.ds(0, 128)], pre_recv.at[h * 2 + pair])

    def attention(h):
        own_col = pl.ds(pl.multiple_of(x * GW + h * 128, 128), 128)

        def for_partner(j, _):
            o, do = attend(h, (1 - y) * 2 + j)
            for i in (0, 1):
                pb[h, j * 2 + i, 0] = o[i * 128 : (i + 1) * 128]
                pb[h, j * 2 + i, 1] = do[i * 128 : (i + 1) * 128]
            return 0

        def for_self(j, _):
            o, do = attend(h, y * 2 + j)
            for i in (0, 1):
                ob[j * 2 + i, y, 0, :, own_col] = o[i * 128 : (i + 1) * 128]
                ob[j * 2 + i, y, 1, :, own_col] = do[i * 128 : (i + 1) * 128]
            return 0

        if h < 2:
            lax.fori_loop(0, 2, for_partner, 0)
            swap(h, 0)
        else:
            for_partner(0, 0)
            for earlier, pair in ((2, 0), (0, 1), (1, 1)):
                swap(earlier, pair)
            for_partner(1, 0)
            swap(2, 1)
        lax.fori_loop(0, 2, for_self, 0)

    def unit(p, part, which, from_x):
        rb, first, rows = PIECES[p]
        skip, width = PARTS[part]
        col = pl.ds(pl.multiple_of(from_x * GW + skip, 128), width)
        group = y if which == 0 else 1 - y
        k = p * 4 + part % 2 * 2 + which
        return ob.at[rb, group, :, pl.ds(first, rows), col], k

    def x_unit(p, part, which):
        src, k = unit(p, part, which, x)
        send(src, src, x_send.at[0], x_recv.at[0, k], right)
        send(src, src, x_send.at[1], x_recv.at[1, k], left)

    def forward(p, part, which):
        src, k = unit(p, part, which, xl)
        wait(src, x_recv.at[0, k])
        send(src.at[0], src.at[0], x_send.at[2], x_recv.at[2, k], right)
        src, k = unit(p, part, which, xr)
        wait(src, x_recv.at[1, k])
        send(src.at[1], src.at[1], x_send.at[3], x_recv.at[3, k], left)

    def arrived(p):
        for which, parts in ((0, (0, 1) if p < 3 else (2,)), (1, (0, 1) if p < 2 else (2,))):
            for part in parts:
                src, k = unit(p, part, which, x)
                wait(src.at[0], x_recv.at[2, k])
                wait(src.at[1], x_recv.at[3, k])

    wait(shard(3).at[z, c], wy_recv.at[3])
    shard_along_z(3)

    wait(recv.at[0, 2], v_recv.at[0])
    wait(recv.at[1, 2], v_recv.at[1])
    sends_q(1)
    wait(sv.at[2], load_sem.at[2])
    sends_v(2)

    shard_to_core(0)
    wait(gall.at[:, z, c], g_recv.at[0])
    for d in (1, 3, 2):
        send(gall.at[:, z, c], gall.at[:, z, c], g_send.at[1], g_recv.at[1], z_peer(d))

    wait(recv.at[0, pl.ds(0, 2)], q_recv.at[0])
    sends_q(2)
    src = shard(0).at[z, c]
    send(src, src, wy_send.at[1], wy_recv.at[1], y_chip(1))
    attention(0)

    shard_to_core(3)
    wait(recv.at[1, pl.ds(0, 2)], q_recv.at[1])
    attention(1)
    x_unit(0, 0, 0)
    x_unit(1, 0, 0)

    wait(gall.at[:, pl.ds(0, 3), c], g_recv.at[1])
    send(gall.at[:, :, c], gall.at[:, :, c], g_send.at[2], g_recv.at[2], other_core)

    wait(recv.at[2, 2], v_recv.at[2])
    wait(recv.at[2, pl.ds(0, 2)], q_recv.at[2])
    attention(2)
    x_unit(0, 1, 0)
    x_unit(1, 1, 0)
    wait(shard(1).at[z, c], wy_recv.at[1])
    shard_along_z(1)
    src = shard(1).at[z, c]
    send(src, src, wy_send.at[2], wy_recv.at[2], y_chip(3))
    forward(0, 0, 0)
    swapped(0, 0)
    swapped(1, 0)
    x_unit(0, 0, 1)
    forward(1, 0, 0)
    wait(shard(2).at[z, c], wy_recv.at[2])
    shard_along_z(2)
    forward(0, 1, 0)
    swapped(2, 0)
    x_unit(0, 1, 1)
    x_unit(1, 0, 1)
    forward(0, 0, 1)
    shard_to_core(1)
    forward(1, 1, 0)
    x_unit(1, 1, 1)
    forward(0, 1, 1)
    x_unit(2, 0, 0)
    x_unit(2, 1, 0)
    forward(1, 0, 1)
    forward(1, 1, 1)
    for h in range(3):
        swapped(h, 1)
    x_unit(2, 2, 1)

    wait(gall.at[:, :, 1 - c], g_recv.at[2])
    moment = time[dp].astype(F32)
    speed = ttan[dp]
    freq = const[1:2, :]
    cos_t, sin_t = jnp.cos(moment * freq), jnp.sin(moment * freq)
    row = lax.broadcasted_iota(jnp.int32, (16, 256), 0)
    emb = jnp.concatenate([cos_t, sin_t], axis=1)
    demb = jnp.concatenate([-freq * sin_t, freq * cos_t], axis=1) * speed
    embs = jnp.where(row == 0, emb, jnp.where(row == 1, demb, 0.0)).astype(BF)
    gates = jnp.dot(embs, gall[...].reshape(256, COLS), preferred_element_type=F32)
    gate, dgate = gates[0:1], gates[1:2]

    for s in (1, 3):
        wait(shard(s).at[:, 1 - c], wc_recv.at[s])
    wait(resv, res_sem)

    def finish(rows, attn, dattn):
        outv[0, rows, :] = (resv[0, rows, :].astype(F32) + gate * attn).astype(BF)
        outv[1, rows, :] = (resv[1, rows, :].astype(F32) + dgate * attn + gate * dattn).astype(BF)
        local(outv.at[0, rows], out.at[rows], out_sem)
        local(outv.at[1, rows], otan.at[rows], out_sem)

    def project(p, yl):
        rb, first, rows = PIECES[p]
        total = None
        for gy in (0, 1):
            term = jnp.dot(
                ob[rb, gy, :, first : first + rows, :].reshape(2 * rows, 1536),
                wall[yl, gy].reshape(1536, COLS),
                preferred_element_type=F32,
            )
            total = term if total is None else total + term
        return total

    def own_piece(p):
        rb, first, rows = PIECES[p]
        total = project(p, y)
        start = pl.multiple_of(y * HALF + rb * 128 + first, 64)
        finish(pl.ds(start, rows), total[:rows], total[rows:])

    for p, (rb, first, rows) in enumerate(PIECES):
        arrived(p)
        total = project(p, 1 - y)
        both = pl.ds(0, 2 * rows)
        po[p, both] = total.astype(BF)
        send(po.at[p, both], pr.at[p, both], y_send.at[p], y_recv.at[p], partner)
        if p == 0:
            forward(2, 0, 0)
            x_unit(3, 2, 0)
            forward(2, 1, 0)
            x_unit(3, 2, 1)
            forward(2, 2, 1)
            shard_to_core(2)
        elif p == 1:
            x_unit(4, 2, 0)
            forward(3, 2, 0)
            x_unit(4, 2, 1)
            forward(3, 2, 1)
            for s in (0, 2):
                wait(shard(s).at[:, 1 - c], wc_recv.at[s])
            own_piece(0)
        elif p == 2:
            forward(4, 2, 0)
            forward(4, 2, 1)
            own_piece(1)
        elif p == 3:
            own_piece(2)
        else:
            own_piece(3)
            own_piece(4)

    for p, (rb, first, rows) in enumerate(PIECES):
        wait(pr.at[p, pl.ds(0, 2 * rows)], y_recv.at[p])
        start = pl.multiple_of((1 - y) * HALF + rb * 128 + first, 64)
        finish(
            pl.ds(start, rows),
            pr[p, 0:rows].astype(F32),
            pr[p, rows : 2 * rows].astype(F32),
        )

    for h in range(3):
        wait(sv.at[h, pl.ds(0, 7)], v_send.at[h])
        wait(sq.at[h, pl.ds(0, 7)], q_send.at[h])
        for pair in (0, 1):
            wait(pb.at[h, pl.ds(pair * 2, 2)], pre_send.at[h * 2 + pair])
    for s in range(4):
        if s > 0:
            wait(shard(0).at[0, 0], wy_send.at[s])
        wait(shard(0).at[pl.ds(0, 3), 0], wz_send.at[s])
        wait(shard(0).at[:, 0], wc_send.at[s])
    wait(gall.at[0, 0, 0], g_send.at[0])
    wait(gall.at[:, pl.ds(0, 3), 0], g_send.at[1])
    wait(gall.at[:, :, 0], g_send.at[2])
    wait(ob.at[:, :, :, :, pl.ds(0, GW)], x_send.at[0])
    wait(ob.at[:, :, :, :, pl.ds(0, GW)], x_send.at[1])
    wait(ob.at[:, :, 0, :, pl.ds(0, GW)], x_send.at[2])
    wait(ob.at[:, :, 1, :, pl.ds(0, GW)], x_send.at[3])
    for p, (_, _, rows) in enumerate(PIECES):
        wait(po.at[p, pl.ds(0, 2 * rows)], y_send.at[p])
    wait(outv, out_sem)


def per_device(
    projections,
    projection_tangent,
    position_ids,
    norm_gain,
    out_weight,
    timestep,
    time_tangent,
    gate_weight,
    residual,
    residual_tangent,
):
    anywhere = pl.BlockSpec(memory_space=pl.ANY)
    dma = pltpu.SemaphoreType.DMA
    shape = jax.ShapeDtypeStruct((SEQ, COLS), BF)
    return pl.pallas_call(
        kernel,
        out_shape=(shape, shape),
        in_specs=[pl.BlockSpec(memory_space=pltpu.HBM)] * 11,
        out_specs=(anywhere, anywhere),
        scratch_shapes=[
            pltpu.VMEM((3, ROWS), jnp.int32),
            pltpu.VMEM((2, ATT_W), F32),
            pltpu.SMEM((16,), jnp.int32),
            pltpu.SMEM((16,), F32),
            pltpu.VMEM((8, 128), F32),
            pltpu.VMEM((2, 2, ROWS, ATT_W), BF),
            pltpu.VMEM((3, 8, ROWS, 256), BF),
            pltpu.VMEM((3, 8, 2, ROWS, 256), BF),
            pltpu.VMEM((3, 3, SEQ, 256), BF),
            pltpu.VMEM((4, 2, 2, ROWS, 1536), BF),
            pltpu.VMEM((3, 4, 2, ROWS, 128), BF),
            pltpu.VMEM((2, 2, 4, 2, 192, COLS), BF),
            pltpu.VMEM((2, 4, 2, 16, COLS), BF),
            pltpu.VMEM((2, SEQ, COLS), BF),
            pltpu.VMEM((2, SEQ, COLS), BF),
            pltpu.VMEM((5, 256, COLS), BF),
            pltpu.VMEM((5, 256, COLS), BF),
            dma((5,)),
            dma((4,)),
            dma,
            dma,
            dma((3,)),
            dma((3,)),
            dma((3,)),
            dma((3,)),
            dma((6,)),
            dma((6,)),
            dma((4,)),
            dma((4,)),
            dma((4,)),
            dma((4,)),
            dma((4,)),
            dma((4,)),
            dma((3,)),
            dma((3,)),
            dma((4,)),
            dma((4, 20)),
            dma((5,)),
            dma((5,)),
        ],
        compiler_params=pltpu.CompilerParams(
            collective_id=0, has_side_effects=True, vmem_limit_bytes=56 * 2**20
        ),
    )(
        projections,
        projection_tangent,
        position_ids.T,
        norm_gain,
        out_weight,
        timestep,
        time_tangent,
        gate_weight,
        residual,
        residual_tangent,
        jnp.asarray(CONST),
    )


def solution(mesh):
    placed = (
        P(None, ("dp", "head"), None),
        P(None, ("dp", "head"), None),
        P(("dp", "head"), None),
        P(),
        P("dp", "head"),
        P(),
        P(),
        P("dp", None),
        P("dp", "head"),
        P("dp", "head"),
    )
    return jax.shard_map(
        per_device,
        mesh=mesh,
        in_specs=placed,
        out_specs=(P("dp", "head"), P("dp", "head")),
        check_vma=False,
    )
```

```python
import math

import jax
import jax.numpy as jnp
import numpy as np
from jax import lax
from jax.experimental import pallas as pl
from jax.experimental.pallas import tpu as pltpu
from jax.sharding import PartitionSpec as P

HEAD_DIM = 128
ATT_W = 3072
EPSILON = 1e-06
MESH = pl.DeviceIdType.MESH
BF = jnp.bfloat16
F32 = jnp.float32

X = 4
ROWS = 128
SEQ = 1024
HALF = 512
GW = 384
COLS = 640
FACTOR = HEAD_DIM ** (-0.5)

PIECES = (
    (0, 0, 128),
    (1, 0, 128),
    (2, 0, 64),
    (2, 64, 64),
    (3, 0, 64),
    (3, 64, 32),
    (3, 96, 32),
)
PARTS = ((0, 256), (256, 128), (0, 384))

ORDER = ((1, 0), (0, 1), (0, 3), (1, 2), (0, 2), (1, 1), (1, 3))


def constants():
    pair_count = HEAD_DIM // 2
    height_pairs = HEAD_DIM // 6
    time_pairs = pair_count - 2 * height_pairs
    j = np.arange(pair_count)
    local = np.where(
        j < time_pairs,
        j,
        np.where(j < time_pairs + height_pairs, j - time_pairs, j - time_pairs - height_pairs),
    )
    span = np.where(j < time_pairs, time_pairs, height_pairs)
    rope = np.repeat(np.power(10000.0, -local / span), 2)
    clock = np.power(10000.0, -np.arange(128) / 128)
    rows = np.zeros((8, 128), np.float32)
    rows[0] = rope
    rows[1] = clock
    return rows, 2 * time_pairs, 2 * (time_pairs + height_pairs)


CONST, LANE_ROW, LANE_COL = constants()


def nt_dot(a, b):
    return lax.dot_general(a, b, (((1,), (1,)), ((), ())), preferred_element_type=F32)


def kernel(
    proj,
    tan,
    pos_hbm,
    gain_hbm,
    wout,
    time_hbm,
    ttan_hbm,
    wgate,
    res,
    rtan,
    const_hbm,
    out,
    otan,
    pos,
    gain,
    time,
    ttan,
    const,
    raw,
    sv,
    sq,
    recv,
    ob,
    pb,
    wall,
    gall,
    resv,
    outv,
    po,
    pr,
    small_sem,
    load_sem,
    res_sem,
    out_sem,
    v_send,
    v_recv,
    q_send,
    q_recv,
    pre_send,
    pre_recv,
    wy_send,
    wy_recv,
    wz_send,
    wz_recv,
    wc_send,
    wc_recv,
    g_send,
    g_recv,
    x_send,
    x_recv,
    f_recv,
    y_send,
    y_recv,
):
    dp = lax.axis_index("dp")
    head = lax.axis_index("head")
    y, x = head // X, lax.rem(head, X)
    yh, z, c = dp // 8, lax.rem(dp // 2, 4), lax.rem(dp, 2)
    partner = {"dp": dp, "head": (1 - y) * X + x}
    right = {"dp": dp, "head": y * X + lax.rem(x + 1, X)}
    left = {"dp": dp, "head": y * X + lax.rem(x + 3, X)}
    xl, xr = lax.rem(x + 3, X), lax.rem(x + 1, X)
    other_core = {"dp": dp + 1 - 2 * c, "head": head}

    def z_peer(d):
        return {"dp": yh * 8 + lax.rem(z + d, 4) * 2 + c, "head": head}

    def send(src, dst, ssem, rsem, to):
        pltpu.make_async_remote_copy(
            src_ref=src,
            dst_ref=dst,
            send_sem=ssem,
            recv_sem=rsem,
            device_id=to,
            device_id_type=MESH,
        ).start()

    def local(src, dst, sem):
        pltpu.make_async_copy(src, dst, sem).start()

    def wait(ref, sem):
        pltpu.make_async_copy(ref, ref, sem).wait()

    def sends_v(h):
        for dy, dx in ORDER:
            g = lax.rem(y + dy, 2) * X + lax.rem(x + dx, X)
            to = {"dp": dp, "head": g}
            send(sv.at[h, g], recv.at[h, 2, mine], v_send, (v_recv if h < 2 else q_recv).at[h], to)
        local(sv.at[h, head], recv.at[h, 2, mine], (v_recv if h < 2 else q_recv).at[h])

    def send_q(h, g):
        to = {"dp": dp, "head": g}
        send(sq.at[h, g], recv.at[h, pl.ds(0, 2), mine], q_send, q_recv.at[h], to)

    def sends_q(h):
        for dy, dx in ORDER:
            send_q(h, lax.rem(y + dy, 2) * X + lax.rem(x + dx, X))
        local(sq.at[h, head], recv.at[h, pl.ds(0, 2), mine], q_recv.at[h])

    def shard(s):
        return wall.at[y if s in (0, 2) else 1 - y, yh if s in (0, 1) else 1 - yh]

    def y_chip(s):
        row = yh if s in (0, 1) else 1 - yh
        return {
            "dp": row * 8 + z * 2 + c,
            "head": (y if s in (0, 2) else 1 - y) * X + x,
        }

    def shard_along_z(s):
        for d in (1, 3, 2):
            src = shard(s).at[z, c]
            send(src, src, wz_send, wz_recv.at[s], z_peer(d))

    def shard_to_core(s):
        wait(shard(s).at[pl.ds(0, 3), c], wz_recv.at[s])
        src = shard(s).at[:, c]
        send(src, src, wc_send, wc_recv.at[s % 2], other_core)

    mine = pl.ds(pl.multiple_of(head * ROWS, ROWS), ROWS)
    gate_cols = wgate.at[:, pl.ds(pl.multiple_of(head * COLS, 128), COLS)]

    for h in range(3):

        def load_v(g, _, h=h):
            col = pl.ds(pl.multiple_of(g * GW + h * 128, 128), 128)
            local(proj.at[2, :, col], sv.at[h, g, :, pl.ds(0, 128)], load_sem.at[0])
            local(tan.at[2, :, col], sv.at[h, g, :, pl.ds(128, 128)], load_sem.at[0])
            return 0

        lax.fori_loop(0, 8, load_v, 0)
    local(wout, shard(0).at[z, c], wy_recv.at[0])
    small = ((pos_hbm, pos), (gain_hbm, gain), (time_hbm, time), (ttan_hbm, ttan), (const_hbm, const))
    for i, (src, dst) in enumerate(small):
        local(src, dst, small_sem.at[i])
    local(proj.at[pl.ds(0, 2)], raw.at[0], load_sem.at[1])
    local(tan.at[pl.ds(0, 2)], raw.at[1], load_sem.at[1])
    local(gate_cols, gall.at[yh, z, c], g_recv.at[0])
    local(res, resv.at[0], res_sem)
    local(rtan, resv.at[1], res_sem)

    barrier = pltpu.get_barrier_semaphore()
    for dy, dx in ORDER:
        to = {"dp": dp, "head": lax.rem(y + dy, 2) * X + lax.rem(x + dx, X)}
        pl.semaphore_signal(barrier, inc=1, device_id=to, device_id_type=MESH)
    for to in (z_peer(1), z_peer(2), z_peer(3), other_core, y_chip(2), y_chip(3)):
        pl.semaphore_signal(barrier, inc=1, device_id=to, device_id_type=MESH)
    pl.semaphore_wait(barrier, 13)

    wait(shard(0).at[z, c], wy_recv.at[0])
    src = shard(0).at[z, c]
    send(src, src, wy_send, wy_recv.at[3], y_chip(3))
    shard_along_z(0)
    wait(sv, load_sem.at[0])
    sends_v(0)
    sends_v(1)
    send(gate_cols, gall.at[yh, z, c], g_send.at[0], g_recv.at[0], y_chip(2))

    for i, (_, dst) in enumerate(small):
        wait(dst, small_sem.at[i])

    line = lax.broadcasted_iota(jnp.int32, (128, ROWS), 0)
    ids = pos[...].astype(F32)
    chosen = jnp.where(
        line < LANE_ROW, ids[0:1, :], jnp.where(line < LANE_COL, ids[1:2, :], ids[2:3, :])
    )
    angle = jnp.transpose(chosen) * const[0:1, :]
    lane = lax.broadcasted_iota(jnp.int32, (ROWS, 128), 1)
    even = lax.rem(lane, 2) == 0
    cosine, sine = jnp.cos(angle), jnp.sin(angle)
    sine = jnp.where(even, -sine, sine)

    def rotate(m):
        swapped = jnp.where(even, pltpu.roll(m, 127, 1), pltpu.roll(m, 1, 1))
        return (m * cosine + swapped * sine).astype(BF)

    wait(raw, load_sem.at[1])
    stats = []
    for a in (0, 1):

        def add(i, carry, a=a):
            square, cross = carry
            col = pl.ds(pl.multiple_of(i * 128, 128), 128)
            q = raw[0, a, :, col].astype(F32)
            dq = raw[1, a, :, col].astype(F32)
            return square + q * q, cross + q * dq

        zero = jnp.zeros((ROWS, 128), F32)
        square, cross = lax.fori_loop(0, ATT_W // 128, add, (zero, zero))
        r = lax.rsqrt(jnp.sum(square, axis=1, keepdims=True) / ATT_W + EPSILON)
        cr = jnp.sum(cross, axis=1, keepdims=True) / ATT_W
        stats.append((r, r * r * r * cr))

    for h in range(3):

        def prepare(i, _, h=h):
            g = lax.rem(y + i // X, 2) * X + lax.rem(x + i, X)
            col = pl.ds(pl.multiple_of(g * GW + h * 128, 128), 128)
            for a in (0, 1):
                r, rc = stats[a]
                q = raw[0, a, :, col].astype(F32)
                dq = raw[1, a, :, col].astype(F32)
                gn = gain[a : a + 1, col]
                n = rotate(q * r * gn)
                dn = rotate(gn * (dq * r - q * rc))
                sq[h, g, a, :, 0:128] = dn if a == 0 else n
                sq[h, g, a, :, 128:256] = n if a == 0 else dn

            if h == 0:

                @pl.when(i > 0)
                def _():
                    send_q(h, g)

            return 0

        lax.fori_loop(0, 8, prepare, 0)
        if h == 0:
            local(sq.at[h, head], recv.at[h, pl.ds(0, 2), mine], q_recv.at[h])

    def attend(h, block):
        rows = pl.ds(pl.multiple_of(block * 256, 256), 256)
        qd = recv[h, 0, rows, :]
        kd = recv[h, 1]
        s = nt_dot(qd[:, 128:], kd[:, :128])
        ds = nt_dot(qd, kd)
        top = jnp.max(s, axis=1, keepdims=True)
        e = jnp.exp2((s - top) * (FACTOR * math.log2(math.e)))
        inv = 1.0 / jnp.sum(e, axis=1, keepdims=True)
        mu = jnp.sum(e * ds, axis=1, keepdims=True) * inv
        t = (e * (ds - mu)).astype(BF)
        vd = recv[h, 2]
        both = jnp.dot(e.astype(BF), vd, preferred_element_type=F32)
        turn = jnp.dot(t, vd[:, :128], preferred_element_type=F32)
        o = both[:, :128] * inv
        do = (both[:, 128:] + turn * FACTOR) * inv
        return o.astype(BF), do.astype(BF)

    def swap(h, pair):
        two = pl.ds(pair * 2, 2)
        col = pl.ds(pl.multiple_of(x * GW + h * 128, 128), 128)
        k = 2 if pair == 1 else h // 2
        send(pb.at[h, two], ob.at[two, y, :, :, col], pre_send, pre_recv.at[k], partner)

    def swapped(k):
        width = (256, 128, 384)[k]
        wait(ob.at[pl.ds(0, 2), 0, :, :, pl.ds(0, width)], pre_recv.at[k])

    def attention(h):
        own_col = pl.ds(pl.multiple_of(x * GW + h * 128, 128), 128)

        def for_partner(j, _):
            o, do = attend(h, (1 - y) * 2 + j)
            for i in (0, 1):
                pb[h, j * 2 + i, 0] = o[i * 128 : (i + 1) * 128]
                pb[h, j * 2 + i, 1] = do[i * 128 : (i + 1) * 128]
            return 0

        def for_self(j, _):
            o, do = attend(h, y * 2 + j)
            for i in (0, 1):
                ob[j * 2 + i, y, 0, :, own_col] = o[i * 128 : (i + 1) * 128]
                ob[j * 2 + i, y, 1, :, own_col] = do[i * 128 : (i + 1) * 128]
            return 0

        if h < 2:
            lax.fori_loop(0, 2, for_partner, 0)
            swap(h, 0)
        else:
            for_partner(0, 0)
            for earlier, pair in ((2, 0), (0, 1), (1, 1)):
                swap(earlier, pair)
            for_partner(1, 0)
            swap(2, 1)
        lax.fori_loop(0, 2, for_self, 0)

    def unit(p, part, which, from_x):
        rb, first, rows = PIECES[p]
        skip, width = PARTS[part]
        col = pl.ds(pl.multiple_of(from_x * GW + skip, 128), width)
        group = y if which == 0 else 1 - y
        k = p * 4 + part * 2 + which if p < 2 else 4 + p * 2 + which
        return ob.at[rb, group, :, pl.ds(first, rows), col], k

    def x_unit(p, part, which):
        src, k = unit(p, part, which, x)
        send(src, src, x_send, x_recv.at[k], right)
        send(src, src, x_send, x_recv.at[k], left)

    def forward(p, part, which):
        rb, first, rows = PIECES[p]
        src, k = unit(p, part, which, xl)
        two = ob.at[rb, :, :, pl.ds(first, rows), pl.ds(0, PARTS[part][1])]
        wait(two, x_recv.at[k])
        send(src.at[0], src.at[0], x_send, f_recv.at[p], right)
        src, k = unit(p, part, which, xr)
        send(src.at[1], src.at[1], x_send, f_recv.at[p], left)

    def arrived(p):
        rb, first, rows = PIECES[p]
        wait(ob.at[rb, :, :, pl.ds(first, rows), pl.ds(0, GW)], f_recv.at[p])

    wait(shard(3).at[z, c], wy_recv.at[3])
    shard_along_z(3)

    wait(recv.at[0, 2], v_recv.at[0])
    wait(recv.at[1, 2], v_recv.at[1])
    sends_q(1)
    sends_v(2)

    shard_to_core(0)
    wait(gall.at[:, z, c], g_recv.at[0])
    for d in (1, 3, 2):
        send(gall.at[:, z, c], gall.at[:, z, c], g_send.at[1], g_recv.at[1], z_peer(d))

    wait(recv.at[0, pl.ds(0, 2)], q_recv.at[0])
    sends_q(2)
    src = shard(0).at[z, c]
    send(src, src, wy_send, wy_recv.at[1], y_chip(1))
    attention(0)

    shard_to_core(3)
    wait(recv.at[1, pl.ds(0, 2)], q_recv.at[1])
    attention(1)
    x_unit(0, 0, 0)
    x_unit(1, 0, 0)

    wait(gall.at[:, pl.ds(0, 3), c], g_recv.at[1])
    send(gall.at[:, :, c], gall.at[:, :, c], g_send.at[2], g_recv.at[2], other_core)

    wait(recv.at[2], q_recv.at[2])
    attention(2)
    x_unit(0, 1, 0)
    x_unit(1, 1, 0)
    wait(shard(1).at[z, c], wy_recv.at[1])
    shard_along_z(1)
    src = shard(1).at[z, c]
    send(src, src, wy_send, wy_recv.at[2], y_chip(3))
    forward(0, 0, 0)
    swapped(0)
    x_unit(0, 0, 1)
    forward(1, 0, 0)
    wait(shard(2).at[z, c], wy_recv.at[2])
    shard_along_z(2)
    forward(0, 1, 0)
    swapped(1)
    x_unit(0, 1, 1)
    x_unit(1, 0, 1)
    forward(0, 0, 1)
    shard_to_core(1)
    forward(1, 1, 0)
    x_unit(1, 1, 1)
    forward(0, 1, 1)
    x_unit(2, 2, 0)
    forward(1, 0, 1)
    forward(1, 1, 1)
    swapped(2)
    x_unit(2, 2, 1)
    x_unit(3, 2, 0)

    wait(gall.at[:, :, 1 - c], g_recv.at[2])
    moment = time[dp].astype(F32)
    speed = ttan[dp]
    freq = const[1:2, :]
    cos_t, sin_t = jnp.cos(moment * freq), jnp.sin(moment * freq)
    row = lax.broadcasted_iota(jnp.int32, (16, 256), 0)
    emb = jnp.concatenate([cos_t, sin_t], axis=1)
    demb = jnp.concatenate([-freq * sin_t, freq * cos_t], axis=1) * speed
    embs = jnp.where(row == 0, emb, jnp.where(row == 1, demb, 0.0)).astype(BF)
    gates = jnp.dot(embs, gall[...].reshape(256, COLS), preferred_element_type=F32)
    gate, dgate = gates[0:1], gates[1:2]

    wait(wall.at[1 - y, :, :, 1 - c], wc_recv.at[1])
    wait(resv, res_sem)

    def finish(rows, attn, dattn):
        outv[0, rows, :] = (resv[0, rows, :].astype(F32) + gate * attn).astype(BF)
        outv[1, rows, :] = (resv[1, rows, :].astype(F32) + dgate * attn + gate * dattn).astype(BF)
        local(outv.at[0, rows], out.at[rows], out_sem)
        local(outv.at[1, rows], otan.at[rows], out_sem)

    def project(rb, first, rows, yl):
        total = None
        for gy in (0, 1):
            term = jnp.dot(
                ob[rb, gy, :, first : first + rows, :].reshape(2 * rows, 1536),
                wall[yl, gy].reshape(1536, COLS),
                preferred_element_type=F32,
            )
            total = term if total is None else total + term
        return total

    def own_block(rb):
        total = project(rb, 0, ROWS, y)
        start = pl.multiple_of(y * HALF + rb * ROWS, ROWS)
        finish(pl.ds(start, ROWS), total[:ROWS], total[ROWS:])

    for p, (rb, first, rows) in enumerate(PIECES):
        arrived(p)
        total = project(rb, first, rows, 1 - y)
        both = pl.ds(0, 2 * rows)
        po[p, both] = total.astype(BF)
        send(po.at[p, both], pr.at[p, both], y_send, y_recv.at[p], partner)
        if p == 0:
            forward(2, 2, 0)
            x_unit(3, 2, 1)
            shard_to_core(2)
        elif p == 1:
            forward(2, 2, 1)
            x_unit(4, 2, 0)
            forward(3, 2, 0)
            x_unit(4, 2, 1)
            wait(wall.at[y, :, :, 1 - c], wc_recv.at[0])
            own_block(0)
        elif p == 2:
            forward(3, 2, 1)
            x_unit(5, 2, 0)
            forward(4, 2, 0)
            x_unit(5, 2, 1)
            own_block(1)
        elif p == 3:
            forward(4, 2, 1)
            x_unit(6, 2, 0)
            forward(5, 2, 0)
            x_unit(6, 2, 1)
        elif p == 4:
            forward(5, 2, 1)
            forward(6, 2, 0)
            forward(6, 2, 1)
            own_block(2)
        elif p == 6:
            own_block(3)

    wait(sv.at[:, pl.ds(0, 7)], v_send)
    wait(sq.at[:, pl.ds(0, 7)], q_send)
    wait(pb, pre_send)
    wait(wall.at[0, 0, pl.ds(0, 3), 0], wy_send)
    wait(wall.at[:, :, pl.ds(0, 3), 0], wz_send)
    wait(wall.at[:, :, :, 0], wc_send)
    wait(gall.at[0, 0, 0], g_send.at[0])
    wait(gall.at[:, pl.ds(0, 3), 0], g_send.at[1])
    wait(gall.at[:, :, 0], g_send.at[2])
    wait(ob.at[:, :, :, :, pl.ds(0, 3 * GW)], x_send)

    for p, (rb, first, rows) in enumerate(PIECES):
        wait(pr.at[p, pl.ds(0, 2 * rows)], y_recv.at[p])
        start = pl.multiple_of((1 - y) * HALF + rb * 128 + first, 32)
        finish(
            pl.ds(start, rows),
            pr[p, 0:rows].astype(F32),
            pr[p, rows : 2 * rows].astype(F32),
        )
    wait(po.at[pl.ds(0, 4)], y_send)
    wait(outv, out_sem)


def copy_kernel(a, b, out_a, out_b, held, load_sem, store_sem):
    parts = []
    for i in range(2):
        rows = pl.ds(i * (SEQ // 2), SEQ // 2)
        for j, (src, dst) in enumerate(((a, out_a), (b, out_b))):
            here = held.at[j, rows]
            load = pltpu.make_async_copy(src.at[rows], here, load_sem.at[j, i])
            load.start()
            parts.append((load, pltpu.make_async_copy(here, dst.at[rows], store_sem)))
    for load, store in parts:
        load.wait()
        store.start()
    pltpu.make_async_copy(held, held, store_sem).wait()


def per_device(
    projections,
    projection_tangent,
    position_ids,
    norm_gain,
    out_weight,
    timestep,
    time_tangent,
    gate_weight,
    residual,
    residual_tangent,
):
    anywhere = pl.BlockSpec(memory_space=pl.ANY)
    dma = pltpu.SemaphoreType.DMA
    shape = jax.ShapeDtypeStruct((SEQ, COLS), BF)
    results = pl.pallas_call(
        kernel,
        out_shape=(shape, shape),
        in_specs=[pl.BlockSpec(memory_space=pltpu.HBM)] * 11,
        out_specs=(anywhere, anywhere),
        scratch_shapes=[
            pltpu.VMEM((3, ROWS), jnp.int32),
            pltpu.VMEM((2, ATT_W), F32),
            pltpu.SMEM((16,), jnp.int32),
            pltpu.SMEM((16,), F32),
            pltpu.VMEM((8, 128), F32),
            pltpu.VMEM((2, 2, ROWS, ATT_W), BF),
            pltpu.VMEM((3, 8, ROWS, 256), BF),
            pltpu.VMEM((3, 8, 2, ROWS, 256), BF),
            pltpu.VMEM((3, 3, SEQ, 256), BF),
            pltpu.VMEM((4, 2, 2, ROWS, 1536), BF),
            pltpu.VMEM((3, 4, 2, ROWS, 128), BF),
            pltpu.VMEM((2, 2, 4, 2, 192, COLS), BF),
            pltpu.VMEM((2, 4, 2, 16, COLS), BF),
            pltpu.VMEM((2, SEQ, COLS), BF),
            pltpu.VMEM((2, SEQ, COLS), BF),
            pltpu.VMEM((7, 256, COLS), BF),
            pltpu.VMEM((7, 256, COLS), BF),
            dma((5,)),
            dma((2,)),
            dma,
            dma,
            dma,
            dma((2,)),
            dma,
            dma((3,)),
            dma,
            dma((3,)),
            dma,
            dma((4,)),
            dma,
            dma((4,)),
            dma,
            dma((2,)),
            dma((3,)),
            dma((3,)),
            dma,
            dma((18,)),
            dma((7,)),
            dma,
            dma((7,)),
        ],
        compiler_params=pltpu.CompilerParams(
            collective_id=0, has_side_effects=True, vmem_limit_bytes=56 * 2**20
        ),
    )(
        projections,
        projection_tangent,
        position_ids.T,
        norm_gain,
        out_weight,
        timestep,
        time_tangent,
        gate_weight,
        residual,
        residual_tangent,
        jnp.asarray(CONST),
    )
    return pl.pallas_call(
        copy_kernel,
        out_shape=(shape, shape),
        in_specs=[anywhere, anywhere],
        out_specs=(anywhere, anywhere),
        scratch_shapes=[pltpu.VMEM((2, SEQ, COLS), BF), dma((2, 2)), dma],
        compiler_params=pltpu.CompilerParams(vmem_limit_bytes=60 * 2**20),
    )(*results)


def solution(mesh):
    placed = (
        P(None, ("dp", "head"), None),
        P(None, ("dp", "head"), None),
        P(("dp", "head"), None),
        P(),
        P("dp", "head"),
        P(),
        P(),
        P("dp", None),
        P("dp", "head"),
        P("dp", "head"),
    )
    return jax.shard_map(
        per_device,
        mesh=mesh,
        in_specs=placed,
        out_specs=(P("dp", "head"), P("dp", "head")),
        check_vma=False,
    )
```

```python
import math

import jax
import jax.numpy as jnp
import numpy as np
from jax import lax
from jax.experimental import pallas as pl
from jax.experimental.pallas import tpu as pltpu
from jax.sharding import PartitionSpec as P

HEAD_DIM = 128
ATT_W = 3072
EPSILON = 1e-06
MESH = pl.DeviceIdType.MESH
BF = jnp.bfloat16
F32 = jnp.float32

X = 4
ROWS = 128
SEQ = 1024
HALF = 512
GW = 384
COLS = 640
FACTOR = HEAD_DIM ** (-0.5)

PIECES = (
    (0, 0, 128),
    (1, 0, 128),
    (2, 0, 64),
    (2, 64, 64),
    (3, 0, 64),
    (3, 64, 32),
    (3, 96, 32),
)
PARTS = ((0, 256), (256, 128), (0, 384))

ORDER = ((1, 0), (0, 1), (0, 3), (1, 2), (0, 2), (1, 1), (1, 3))


def constants():
    pair_count = HEAD_DIM // 2
    height_pairs = HEAD_DIM // 6
    time_pairs = pair_count - 2 * height_pairs
    j = np.arange(pair_count)
    local = np.where(
        j < time_pairs,
        j,
        np.where(j < time_pairs + height_pairs, j - time_pairs, j - time_pairs - height_pairs),
    )
    span = np.where(j < time_pairs, time_pairs, height_pairs)
    rope = np.repeat(np.power(10000.0, -local / span), 2)
    clock = np.power(10000.0, -np.arange(128) / 128)
    rows = np.zeros((8, 128), np.float32)
    rows[0] = rope
    rows[1] = clock
    return rows, 2 * time_pairs, 2 * (time_pairs + height_pairs)


CONST, LANE_ROW, LANE_COL = constants()


def nt_dot(a, b):
    return lax.dot_general(a, b, (((1,), (1,)), ((), ())), preferred_element_type=F32)


def kernel(
    proj,
    tan,
    pos_hbm,
    gain_hbm,
    wout,
    time_hbm,
    ttan_hbm,
    wgate,
    res,
    rtan,
    const_hbm,
    out,
    otan,
    pos,
    gain,
    time,
    ttan,
    const,
    raw,
    sv,
    sq,
    recv,
    ob,
    pb,
    wall,
    gall,
    resv,
    po,
    pr,
    small_sem,
    load_sem,
    res_sem,
    v_send,
    v_recv,
    q_send,
    q_recv,
    pre_send,
    pre_recv,
    wy_send,
    wy_recv,
    wz_send,
    wz_recv,
    wc_send,
    wc_recv,
    g_send,
    g_recv,
    x_send,
    x_recv,
    f_recv,
    y_send,
    y_recv,
):
    dp = lax.axis_index("dp")
    head = lax.axis_index("head")
    y, x = head // X, lax.rem(head, X)
    yh, z, c = dp // 8, lax.rem(dp // 2, 4), lax.rem(dp, 2)
    partner = {"dp": dp, "head": (1 - y) * X + x}
    right = {"dp": dp, "head": y * X + lax.rem(x + 1, X)}
    left = {"dp": dp, "head": y * X + lax.rem(x + 3, X)}
    xl, xr = lax.rem(x + 3, X), lax.rem(x + 1, X)
    other_core = {"dp": dp + 1 - 2 * c, "head": head}

    def z_peer(d):
        return {"dp": yh * 8 + lax.rem(z + d, 4) * 2 + c, "head": head}

    def send(src, dst, ssem, rsem, to):
        pltpu.make_async_remote_copy(
            src_ref=src,
            dst_ref=dst,
            send_sem=ssem,
            recv_sem=rsem,
            device_id=to,
            device_id_type=MESH,
        ).start()

    def local(src, dst, sem):
        pltpu.make_async_copy(src, dst, sem).start()

    def wait(ref, sem):
        pltpu.make_async_copy(ref, ref, sem).wait()

    def sends_v(h):
        for dy, dx in ORDER:
            g = lax.rem(y + dy, 2) * X + lax.rem(x + dx, X)
            to = {"dp": dp, "head": g}
            send(sv.at[h, g], recv.at[h, 2, mine], v_send, (v_recv if h < 2 else q_recv).at[h], to)
        local(sv.at[h, head], recv.at[h, 2, mine], (v_recv if h < 2 else q_recv).at[h])

    def send_q(h, g):
        to = {"dp": dp, "head": g}
        send(sq.at[h, g], recv.at[h, pl.ds(0, 2), mine], q_send, q_recv.at[h], to)

    def sends_q(h):
        for dy, dx in ORDER:
            send_q(h, lax.rem(y + dy, 2) * X + lax.rem(x + dx, X))
        local(sq.at[h, head], recv.at[h, pl.ds(0, 2), mine], q_recv.at[h])

    def shard(s):
        return wall.at[y if s in (0, 2) else 1 - y, yh if s in (0, 1) else 1 - yh]

    def y_chip(s):
        row = yh if s in (0, 1) else 1 - yh
        return {
            "dp": row * 8 + z * 2 + c,
            "head": (y if s in (0, 2) else 1 - y) * X + x,
        }

    def shard_along_z(s):
        for d in (1, 3, 2):
            src = shard(s).at[z, c]
            send(src, src, wz_send, wz_recv.at[s], z_peer(d))

    def shard_to_core(s):
        wait(shard(s).at[pl.ds(0, 3), c], wz_recv.at[s])
        src = shard(s).at[:, c]
        send(src, src, wc_send, wc_recv.at[s % 2], other_core)

    mine = pl.ds(pl.multiple_of(head * ROWS, ROWS), ROWS)
    gate_cols = wgate.at[:, pl.ds(pl.multiple_of(head * COLS, 128), COLS)]

    barrier = pltpu.get_barrier_semaphore()
    for dy, dx in ORDER:
        to = {"dp": dp, "head": lax.rem(y + dy, 2) * X + lax.rem(x + dx, X)}
        pl.semaphore_signal(barrier, inc=1, device_id=to, device_id_type=MESH)
    for to in (z_peer(1), z_peer(2), z_peer(3), other_core, y_chip(2), y_chip(3)):
        pl.semaphore_signal(barrier, inc=1, device_id=to, device_id_type=MESH)

    for h in range(3):

        def load_v(g, _, h=h):
            col = pl.ds(pl.multiple_of(g * GW + h * 128, 128), 128)
            local(proj.at[2, :, col], sv.at[h, g, :, pl.ds(0, 128)], load_sem.at[0])
            local(tan.at[2, :, col], sv.at[h, g, :, pl.ds(128, 128)], load_sem.at[0])
            return 0

        lax.fori_loop(0, 8, load_v, 0)
    local(wout, shard(0).at[z, c], wy_recv.at[0])
    small = ((pos_hbm, pos), (gain_hbm, gain), (time_hbm, time), (ttan_hbm, ttan), (const_hbm, const))
    for i, (src, dst) in enumerate(small):
        local(src, dst, small_sem.at[i])
    local(proj.at[pl.ds(0, 2)], raw.at[0], load_sem.at[1])
    local(tan.at[pl.ds(0, 2)], raw.at[1], load_sem.at[1])
    local(gate_cols, gall.at[yh, z, c], g_recv.at[0])
    local(res, resv.at[0], res_sem)
    local(rtan, resv.at[1], res_sem)

    pl.semaphore_wait(barrier, 13)

    wait(shard(0).at[z, c], wy_recv.at[0])
    src = shard(0).at[z, c]
    send(src, src, wy_send, wy_recv.at[3], y_chip(3))
    shard_along_z(0)
    wait(sv, load_sem.at[0])
    sends_v(0)
    sends_v(1)
    send(gate_cols, gall.at[yh, z, c], g_send.at[0], g_recv.at[0], y_chip(2))

    for i, (_, dst) in enumerate(small):
        wait(dst, small_sem.at[i])

    line = lax.broadcasted_iota(jnp.int32, (128, ROWS), 0)
    ids = pos[...].astype(F32)
    chosen = jnp.where(
        line < LANE_ROW, ids[0:1, :], jnp.where(line < LANE_COL, ids[1:2, :], ids[2:3, :])
    )
    angle = jnp.transpose(chosen) * const[0:1, :]
    lane = lax.broadcasted_iota(jnp.int32, (ROWS, 128), 1)
    even = lax.rem(lane, 2) == 0
    cosine, sine = jnp.cos(angle), jnp.sin(angle)
    sine = jnp.where(even, -sine, sine)

    def rotate(m):
        swapped = jnp.where(even, pltpu.roll(m, 127, 1), pltpu.roll(m, 1, 1))
        return (m * cosine + swapped * sine).astype(BF)

    wait(raw, load_sem.at[1])
    stats = []
    for a in (0, 1):

        def add(i, carry, a=a):
            square, cross = carry
            col = pl.ds(pl.multiple_of(i * 128, 128), 128)
            q = raw[0, a, :, col].astype(F32)
            dq = raw[1, a, :, col].astype(F32)
            return square + q * q, cross + q * dq

        zero = jnp.zeros((ROWS, 128), F32)
        square, cross = lax.fori_loop(0, ATT_W // 128, add, (zero, zero))
        r = lax.rsqrt(jnp.sum(square, axis=1, keepdims=True) / ATT_W + EPSILON)
        cr = jnp.sum(cross, axis=1, keepdims=True) / ATT_W
        stats.append((r, r * r * r * cr))

    for h in range(3):

        def prepare(i, _, h=h):
            g = lax.rem(y + i // X, 2) * X + lax.rem(x + i, X)
            col = pl.ds(pl.multiple_of(g * GW + h * 128, 128), 128)
            for a in (0, 1):
                r, rc = stats[a]
                q = raw[0, a, :, col].astype(F32)
                dq = raw[1, a, :, col].astype(F32)
                gn = gain[a : a + 1, col]
                n = rotate(q * r * gn)
                dn = rotate(gn * (dq * r - q * rc))
                sq[h, g, a, :, 0:128] = dn if a == 0 else n
                sq[h, g, a, :, 128:256] = n if a == 0 else dn

            if h == 0:

                @pl.when(i > 0)
                def _():
                    send_q(h, g)

            return 0

        lax.fori_loop(0, 8, prepare, 0)
        if h == 0:
            local(sq.at[h, head], recv.at[h, pl.ds(0, 2), mine], q_recv.at[h])

    def attend(h, block):
        rows = pl.ds(pl.multiple_of(block * 256, 256), 256)
        qd = recv[h, 0, rows, :]
        kd = recv[h, 1]
        s = nt_dot(qd[:, 128:], kd[:, :128])
        ds = nt_dot(qd, kd)
        top = jnp.max(s, axis=1, keepdims=True)
        e = jnp.exp2((s - top) * (FACTOR * math.log2(math.e)))
        inv = 1.0 / jnp.sum(e, axis=1, keepdims=True)
        mu = jnp.sum(e * ds, axis=1, keepdims=True) * inv
        t = (e * (ds - mu)).astype(BF)
        vd = recv[h, 2]
        both = jnp.dot(e.astype(BF), vd, preferred_element_type=F32)
        turn = jnp.dot(t, vd[:, :128], preferred_element_type=F32)
        o = both[:, :128] * inv
        do = (both[:, 128:] + turn * FACTOR) * inv
        return o.astype(BF), do.astype(BF)

    def swap(h, pair):
        two = pl.ds(pair * 2, 2)
        col = pl.ds(pl.multiple_of(x * GW + h * 128, 128), 128)
        k = 2 if pair == 1 else h // 2
        send(pb.at[h, two], ob.at[two, y, :, :, col], pre_send, pre_recv.at[k], partner)

    def swapped(k):
        width = (256, 128, 384)[k]
        wait(ob.at[pl.ds(0, 2), 0, :, :, pl.ds(0, width)], pre_recv.at[k])

    def attention(h):
        own_col = pl.ds(pl.multiple_of(x * GW + h * 128, 128), 128)

        def for_partner(j, _):
            o, do = attend(h, (1 - y) * 2 + j)
            for i in (0, 1):
                pb[h, j * 2 + i, 0] = o[i * 128 : (i + 1) * 128]
                pb[h, j * 2 + i, 1] = do[i * 128 : (i + 1) * 128]
            return 0

        def for_self(j, _):
            o, do = attend(h, y * 2 + j)
            for i in (0, 1):
                ob[j * 2 + i, y, 0, :, own_col] = o[i * 128 : (i + 1) * 128]
                ob[j * 2 + i, y, 1, :, own_col] = do[i * 128 : (i + 1) * 128]
            return 0

        if h < 2:
            lax.fori_loop(0, 2, for_partner, 0)
            swap(h, 0)
        else:
            for_partner(0, 0)
            for earlier, pair in ((2, 0), (0, 1), (1, 1)):
                swap(earlier, pair)
            for_partner(1, 0)
            swap(2, 1)
        lax.fori_loop(0, 2, for_self, 0)

    def unit(p, part, which, from_x):
        rb, first, rows = PIECES[p]
        skip, width = PARTS[part]
        col = pl.ds(pl.multiple_of(from_x * GW + skip, 128), width)
        group = y if which == 0 else 1 - y
        k = p * 4 + part * 2 + which if p < 2 else 4 + p * 2 + which
        return ob.at[rb, group, :, pl.ds(first, rows), col], k

    def x_unit(p, part, which):
        src, k = unit(p, part, which, x)
        send(src, src, x_send, x_recv.at[k], right)
        send(src, src, x_send, x_recv.at[k], left)

    def forward(p, part, which):
        rb, first, rows = PIECES[p]
        src, k = unit(p, part, which, xl)
        two = ob.at[rb, :, :, pl.ds(first, rows), pl.ds(0, PARTS[part][1])]
        wait(two, x_recv.at[k])
        send(src.at[0], src.at[0], x_send, f_recv.at[p], right)
        src, k = unit(p, part, which, xr)
        send(src.at[1], src.at[1], x_send, f_recv.at[p], left)

    def arrived(p):
        rb, first, rows = PIECES[p]
        wait(ob.at[rb, :, :, pl.ds(first, rows), pl.ds(0, GW)], f_recv.at[p])

    wait(shard(3).at[z, c], wy_recv.at[3])
    shard_along_z(3)

    wait(recv.at[0, 2], v_recv.at[0])
    wait(recv.at[1, 2], v_recv.at[1])
    sends_q(1)
    sends_v(2)

    shard_to_core(0)
    wait(gall.at[:, z, c], g_recv.at[0])
    for d in (1, 3, 2):
        send(gall.at[:, z, c], gall.at[:, z, c], g_send.at[1], g_recv.at[1], z_peer(d))

    wait(recv.at[0, pl.ds(0, 2)], q_recv.at[0])
    sends_q(2)
    src = shard(0).at[z, c]
    send(src, src, wy_send, wy_recv.at[1], y_chip(1))
    attention(0)

    shard_to_core(3)
    wait(recv.at[1, pl.ds(0, 2)], q_recv.at[1])
    attention(1)
    x_unit(0, 0, 0)
    x_unit(1, 0, 0)

    wait(gall.at[:, pl.ds(0, 3), c], g_recv.at[1])
    send(gall.at[:, :, c], gall.at[:, :, c], g_send.at[2], g_recv.at[2], other_core)

    wait(recv.at[2], q_recv.at[2])
    attention(2)
    x_unit(0, 1, 0)
    x_unit(1, 1, 0)
    wait(shard(1).at[z, c], wy_recv.at[1])
    shard_along_z(1)
    src = shard(1).at[z, c]
    send(src, src, wy_send, wy_recv.at[2], y_chip(3))
    forward(0, 0, 0)
    forward(1, 0, 0)
    x_unit(2, 2, 0)
    swapped(0)
    x_unit(0, 0, 1)
    wait(shard(2).at[z, c], wy_recv.at[2])
    shard_along_z(2)
    forward(0, 1, 0)
    swapped(1)
    x_unit(0, 1, 1)
    x_unit(1, 0, 1)
    forward(0, 0, 1)
    shard_to_core(1)
    forward(1, 1, 0)
    x_unit(1, 1, 1)
    forward(0, 1, 1)
    forward(1, 0, 1)
    forward(1, 1, 1)
    swapped(2)
    x_unit(2, 2, 1)
    x_unit(3, 2, 0)

    wait(gall.at[:, :, 1 - c], g_recv.at[2])
    moment = time[dp].astype(F32)
    speed = ttan[dp]
    freq = const[1:2, :]
    cos_t, sin_t = jnp.cos(moment * freq), jnp.sin(moment * freq)
    row = lax.broadcasted_iota(jnp.int32, (16, 256), 0)
    emb = jnp.concatenate([cos_t, sin_t], axis=1)
    demb = jnp.concatenate([-freq * sin_t, freq * cos_t], axis=1) * speed
    embs = jnp.where(row == 0, emb, jnp.where(row == 1, demb, 0.0)).astype(BF)
    gates = jnp.dot(embs, gall[...].reshape(256, COLS), preferred_element_type=F32)
    gate, dgate = gates[0:1], gates[1:2]

    wait(wall.at[1 - y, :, :, 1 - c], wc_recv.at[1])
    wait(resv, res_sem)

    def finish(rows, attn, dattn):
        out[rows, :] = (resv[0, rows, :].astype(F32) + gate * attn).astype(BF)
        otan[rows, :] = (resv[1, rows, :].astype(F32) + dgate * attn + gate * dattn).astype(BF)

    def project(rb, first, rows, yl):
        total = None
        for gy in (0, 1):
            term = jnp.dot(
                ob[rb, gy, :, first : first + rows, :].reshape(2 * rows, 1536),
                wall[yl, gy].reshape(1536, COLS),
                preferred_element_type=F32,
            )
            total = term if total is None else total + term
        return total

    def own_block(rb):
        total = project(rb, 0, ROWS, y)
        start = pl.multiple_of(y * HALF + rb * ROWS, ROWS)
        finish(pl.ds(start, ROWS), total[:ROWS], total[ROWS:])

    for p, (rb, first, rows) in enumerate(PIECES):
        arrived(p)
        total = project(rb, first, rows, 1 - y)
        both = pl.ds(0, 2 * rows)
        po[p, both] = total.astype(BF)
        send(po.at[p, both], pr.at[p, both], y_send, y_recv.at[p], partner)
        if p == 0:
            forward(2, 2, 0)
            x_unit(3, 2, 1)
            shard_to_core(2)
        elif p == 1:
            forward(2, 2, 1)
            x_unit(4, 2, 0)
            forward(3, 2, 0)
            x_unit(4, 2, 1)
            wait(wall.at[y, :, :, 1 - c], wc_recv.at[0])
            own_block(0)
        elif p == 2:
            forward(3, 2, 1)
            x_unit(5, 2, 0)
            forward(4, 2, 0)
            x_unit(5, 2, 1)
            own_block(1)
        elif p == 3:
            forward(4, 2, 1)
            x_unit(6, 2, 0)
            forward(5, 2, 0)
            x_unit(6, 2, 1)
        elif p == 4:
            forward(5, 2, 1)
            forward(6, 2, 0)
            forward(6, 2, 1)
            own_block(2)
        elif p == 6:
            own_block(3)

    wait(sv.at[:, pl.ds(0, 7)], v_send)
    wait(sq.at[:, pl.ds(0, 7)], q_send)
    wait(pb, pre_send)
    wait(wall.at[0, 0, pl.ds(0, 3), 0], wy_send)
    wait(wall.at[:, :, pl.ds(0, 3), 0], wz_send)
    wait(wall.at[:, :, :, 0], wc_send)
    wait(gall.at[0, 0, 0], g_send.at[0])
    wait(gall.at[:, pl.ds(0, 3), 0], g_send.at[1])
    wait(gall.at[:, :, 0], g_send.at[2])
    wait(ob.at[:, :, :, :, pl.ds(0, 3 * GW)], x_send)

    for p, (rb, first, rows) in enumerate(PIECES):
        wait(pr.at[p, pl.ds(0, 2 * rows)], y_recv.at[p])
        start = pl.multiple_of((1 - y) * HALF + rb * 128 + first, 32)
        finish(
            pl.ds(start, rows),
            pr[p, 0:rows].astype(F32),
            pr[p, rows : 2 * rows].astype(F32),
        )
    wait(po.at[pl.ds(0, 4)], y_send)


def copy_kernel(a, b, out_a, out_b, sem):
    copies = []
    for i in range(2):
        rows = pl.ds(i * (SEQ // 2), SEQ // 2)
        for j, (src, dst) in enumerate(((a, out_a), (b, out_b))):
            copies.append(pltpu.make_async_copy(src.at[rows], dst.at[rows], sem.at[j, i]))
    for copy in copies:
        copy.start()
    for copy in copies:
        copy.wait()


def per_device(
    projections,
    projection_tangent,
    position_ids,
    norm_gain,
    out_weight,
    timestep,
    time_tangent,
    gate_weight,
    residual,
    residual_tangent,
):
    anywhere = pl.BlockSpec(memory_space=pl.ANY)
    dma = pltpu.SemaphoreType.DMA
    shape = jax.ShapeDtypeStruct((SEQ, COLS), BF)
    results = pl.pallas_call(
        kernel,
        out_shape=(pltpu.VMEM((SEQ, COLS), BF),) * 2,
        in_specs=[pl.BlockSpec(memory_space=pltpu.HBM)] * 11,
        out_specs=(pl.BlockSpec(memory_space=pltpu.VMEM),) * 2,
        scratch_shapes=[
            pltpu.VMEM((3, ROWS), jnp.int32),
            pltpu.VMEM((2, ATT_W), F32),
            pltpu.SMEM((16,), jnp.int32),
            pltpu.SMEM((16,), F32),
            pltpu.VMEM((8, 128), F32),
            pltpu.VMEM((2, 2, ROWS, ATT_W), BF),
            pltpu.VMEM((3, 8, ROWS, 256), BF),
            pltpu.VMEM((3, 8, 2, ROWS, 256), BF),
            pltpu.VMEM((3, 3, SEQ, 256), BF),
            pltpu.VMEM((4, 2, 2, ROWS, 1536), BF),
            pltpu.VMEM((3, 4, 2, ROWS, 128), BF),
            pltpu.VMEM((2, 2, 4, 2, 192, COLS), BF),
            pltpu.VMEM((2, 4, 2, 16, COLS), BF),
            pltpu.VMEM((2, SEQ, COLS), BF),
            pltpu.VMEM((7, 256, COLS), BF),
            pltpu.VMEM((7, 256, COLS), BF),
            dma((5,)),
            dma((2,)),
            dma,
            dma,
            dma((2,)),
            dma,
            dma((3,)),
            dma,
            dma((3,)),
            dma,
            dma((4,)),
            dma,
            dma((4,)),
            dma,
            dma((2,)),
            dma((3,)),
            dma((3,)),
            dma,
            dma((18,)),
            dma((7,)),
            dma,
            dma((7,)),
        ],
        compiler_params=pltpu.CompilerParams(
            collective_id=0, has_side_effects=True, vmem_limit_bytes=56 * 2**20
        ),
    )(
        projections,
        projection_tangent,
        position_ids.T,
        norm_gain,
        out_weight,
        timestep,
        time_tangent,
        gate_weight,
        residual,
        residual_tangent,
        jnp.asarray(CONST),
    )
    return pl.pallas_call(
        copy_kernel,
        out_shape=(shape, shape),
        in_specs=[anywhere, anywhere],
        out_specs=(anywhere, anywhere),
        scratch_shapes=[dma((2, 2))],
        compiler_params=pltpu.CompilerParams(vmem_limit_bytes=8 * 2**20),
    )(*results)


def solution(mesh):
    placed = (
        P(None, ("dp", "head"), None),
        P(None, ("dp", "head"), None),
        P(("dp", "head"), None),
        P(),
        P("dp", "head"),
        P(),
        P(),
        P("dp", None),
        P("dp", "head"),
        P("dp", "head"),
    )
    return jax.shard_map(
        per_device,
        mesh=mesh,
        in_specs=placed,
        out_specs=(P("dp", "head"), P("dp", "head")),
        check_vma=False,
    )
```

```python
import math

import jax
import jax.numpy as jnp
import numpy as np
from jax import lax
from jax.experimental import pallas as pl
from jax.experimental.pallas import tpu as pltpu
from jax.sharding import PartitionSpec as P

HEAD_DIM = 128
ATT_W = 3072
EPSILON = 1e-06
MESH = pl.DeviceIdType.MESH
BF = jnp.bfloat16
F32 = jnp.float32

X = 4
ROWS = 128
SEQ = 1024
HALF = 512
GW = 384
COLS = 640
FACTOR = HEAD_DIM ** (-0.5)

PIECES = (
    (0, 0, 128),
    (1, 0, 128),
    (2, 0, 64),
    (2, 64, 64),
    (3, 0, 64),
    (3, 64, 32),
    (3, 96, 32),
)
ALL = 5
PARTS = ((0, 256), (256, 128), (0, 384))

ORDER = ((1, 0), (0, 1), (0, 3), (1, 2), (0, 2), (1, 1), (1, 3))


def constants():
    pair_count = HEAD_DIM // 2
    height_pairs = HEAD_DIM // 6
    time_pairs = pair_count - 2 * height_pairs
    j = np.arange(pair_count)
    local = np.where(
        j < time_pairs,
        j,
        np.where(j < time_pairs + height_pairs, j - time_pairs, j - time_pairs - height_pairs),
    )
    span = np.where(j < time_pairs, time_pairs, height_pairs)
    rope = np.repeat(np.power(10000.0, -local / span), 2)
    clock = np.power(10000.0, -np.arange(128) / 128)
    rows = np.zeros((8, 128), np.float32)
    rows[0] = rope
    rows[1] = clock
    return rows, 2 * time_pairs, 2 * (time_pairs + height_pairs)


CONST, LANE_ROW, LANE_COL = constants()


def nt_dot(a, b):
    return lax.dot_general(a, b, (((1,), (1,)), ((), ())), preferred_element_type=F32)


def kernel(
    proj,
    tan,
    pos_hbm,
    gain_hbm,
    wout,
    time_hbm,
    ttan_hbm,
    wgate,
    res,
    rtan,
    const_hbm,
    out,
    otan,
    pos,
    gain,
    time,
    ttan,
    const,
    raw,
    sv,
    sq,
    recv,
    ob,
    pb,
    wall,
    gall,
    resv,
    po,
    pr,
    small_sem,
    load_sem,
    res_sem,
    v_send,
    v_recv,
    q_send,
    q_recv,
    pre_send,
    pre_recv,
    wy_send,
    wy_recv,
    wz_send,
    wz_recv,
    wc_send,
    wc_recv,
    g_send,
    g_recv,
    x_send,
    x_recv,
    f_recv,
    y_send,
    y_recv,
):
    dp = lax.axis_index("dp")
    head = lax.axis_index("head")
    y, x = head // X, lax.rem(head, X)
    yh, z, c = dp // 8, lax.rem(dp // 2, 4), lax.rem(dp, 2)
    partner = {"dp": dp, "head": (1 - y) * X + x}
    right = {"dp": dp, "head": y * X + lax.rem(x + 1, X)}
    left = {"dp": dp, "head": y * X + lax.rem(x + 3, X)}
    xl, xr = lax.rem(x + 3, X), lax.rem(x + 1, X)
    other_core = {"dp": dp + 1 - 2 * c, "head": head}

    def z_peer(d):
        return {"dp": yh * 8 + lax.rem(z + d, 4) * 2 + c, "head": head}

    def send(src, dst, ssem, rsem, to):
        pltpu.make_async_remote_copy(
            src_ref=src,
            dst_ref=dst,
            send_sem=ssem,
            recv_sem=rsem,
            device_id=to,
            device_id_type=MESH,
        ).start()

    def local(src, dst, sem):
        pltpu.make_async_copy(src, dst, sem).start()

    def wait(ref, sem):
        pltpu.make_async_copy(ref, ref, sem).wait()

    def sends_v(h):
        for dy, dx in ORDER:
            g = lax.rem(y + dy, 2) * X + lax.rem(x + dx, X)
            to = {"dp": dp, "head": g}
            send(sv.at[h, g], recv.at[h, 2, mine], v_send, (v_recv if h < 2 else q_recv).at[h], to)
        local(sv.at[h, head], recv.at[h, 2, mine], (v_recv if h < 2 else q_recv).at[h])

    def send_q(h, g):
        to = {"dp": dp, "head": g}
        send(sq.at[h, g], recv.at[h, pl.ds(0, 2), mine], q_send, q_recv.at[h], to)

    def sends_q(h):
        for dy, dx in ORDER:
            send_q(h, lax.rem(y + dy, 2) * X + lax.rem(x + dx, X))
        local(sq.at[h, head], recv.at[h, pl.ds(0, 2), mine], q_recv.at[h])

    def shard(s):
        return wall.at[y if s in (0, 2) else 1 - y, yh if s in (0, 1) else 1 - yh]

    def y_chip(s):
        row = yh if s in (0, 1) else 1 - yh
        return {
            "dp": row * 8 + z * 2 + c,
            "head": (y if s in (0, 2) else 1 - y) * X + x,
        }

    def shard_along_z(s):
        for d in (1, 3, 2):
            src = shard(s).at[z, c]
            send(src, src, wz_send, wz_recv.at[s], z_peer(d))

    def shard_to_core(s):
        wait(shard(s).at[pl.ds(0, 3), c], wz_recv.at[s])
        src = shard(s).at[:, c]
        send(src, src, wc_send, wc_recv.at[s % 2], other_core)

    mine = pl.ds(pl.multiple_of(head * ROWS, ROWS), ROWS)
    gate_cols = wgate.at[:, pl.ds(pl.multiple_of(head * COLS, 128), COLS)]

    barrier = pltpu.get_barrier_semaphore()
    for dy, dx in ORDER:
        to = {"dp": dp, "head": lax.rem(y + dy, 2) * X + lax.rem(x + dx, X)}
        pl.semaphore_signal(barrier, inc=1, device_id=to, device_id_type=MESH)
    for to in (z_peer(1), z_peer(2), z_peer(3), other_core, y_chip(2), y_chip(3)):
        pl.semaphore_signal(barrier, inc=1, device_id=to, device_id_type=MESH)

    for h in range(3):

        def load_v(g, _, h=h):
            col = pl.ds(pl.multiple_of(g * GW + h * 128, 128), 128)
            local(proj.at[2, :, col], sv.at[h, g, :, pl.ds(0, 128)], load_sem.at[0])
            local(tan.at[2, :, col], sv.at[h, g, :, pl.ds(128, 128)], load_sem.at[0])
            return 0

        lax.fori_loop(0, 8, load_v, 0)
    local(wout, shard(0).at[z, c], wy_recv.at[0])
    small = ((pos_hbm, pos), (gain_hbm, gain), (time_hbm, time), (ttan_hbm, ttan), (const_hbm, const))
    for i, (src, dst) in enumerate(small):
        local(src, dst, small_sem.at[i])
    local(proj.at[pl.ds(0, 2)], raw.at[0], load_sem.at[1])
    local(tan.at[pl.ds(0, 2)], raw.at[1], load_sem.at[1])
    local(gate_cols, gall.at[yh, z, c], g_recv.at[0])
    local(res, resv.at[0], res_sem)
    local(rtan, resv.at[1], res_sem)

    pl.semaphore_wait(barrier, 13)

    wait(shard(0).at[z, c], wy_recv.at[0])
    src = shard(0).at[z, c]
    send(src, src, wy_send, wy_recv.at[3], y_chip(3))
    shard_along_z(0)
    wait(sv, load_sem.at[0])
    sends_v(0)
    sends_v(1)
    send(gate_cols, gall.at[yh, z, c], g_send.at[0], g_recv.at[0], y_chip(2))

    for i, (_, dst) in enumerate(small):
        wait(dst, small_sem.at[i])

    line = lax.broadcasted_iota(jnp.int32, (128, ROWS), 0)
    ids = pos[...].astype(F32)
    chosen = jnp.where(
        line < LANE_ROW, ids[0:1, :], jnp.where(line < LANE_COL, ids[1:2, :], ids[2:3, :])
    )
    angle = jnp.transpose(chosen) * const[0:1, :]
    lane = lax.broadcasted_iota(jnp.int32, (ROWS, 128), 1)
    even = lax.rem(lane, 2) == 0
    cosine, sine = jnp.cos(angle), jnp.sin(angle)
    sine = jnp.where(even, -sine, sine)

    def rotate(m):
        swapped = jnp.where(even, pltpu.roll(m, 127, 1), pltpu.roll(m, 1, 1))
        return (m * cosine + swapped * sine).astype(BF)

    wait(raw, load_sem.at[1])
    stats = []
    for a in (0, 1):

        def add(i, carry, a=a):
            square, cross = carry
            col = pl.ds(pl.multiple_of(i * 128, 128), 128)
            q = raw[0, a, :, col].astype(F32)
            dq = raw[1, a, :, col].astype(F32)
            return square + q * q, cross + q * dq

        zero = jnp.zeros((ROWS, 128), F32)
        square, cross = lax.fori_loop(0, ATT_W // 128, add, (zero, zero))
        r = lax.rsqrt(jnp.sum(square, axis=1, keepdims=True) / ATT_W + EPSILON)
        cr = jnp.sum(cross, axis=1, keepdims=True) / ATT_W
        stats.append((r, r * r * r * cr))

    for h in range(3):

        def prepare(i, _, h=h):
            g = lax.rem(y + i // X, 2) * X + lax.rem(x + i, X)
            col = pl.ds(pl.multiple_of(g * GW + h * 128, 128), 128)
            for a in (0, 1):
                r, rc = stats[a]
                q = raw[0, a, :, col].astype(F32)
                dq = raw[1, a, :, col].astype(F32)
                gn = gain[a : a + 1, col]
                n = rotate(q * r * gn)
                dn = rotate(gn * (dq * r - q * rc))
                sq[h, g, a, :, 0:128] = dn if a == 0 else n
                sq[h, g, a, :, 128:256] = n if a == 0 else dn

            if h == 0:

                @pl.when(i > 0)
                def _():
                    send_q(h, g)

            return 0

        lax.fori_loop(0, 8, prepare, 0)
        if h == 0:
            local(sq.at[h, head], recv.at[h, pl.ds(0, 2), mine], q_recv.at[h])

    def attend(h, block):
        rows = pl.ds(pl.multiple_of(block * 256, 256), 256)
        qd = recv[h, 0, rows, :]
        kd = recv[h, 1]
        s = nt_dot(qd[:, 128:], kd[:, :128])
        ds = nt_dot(qd, kd)
        top = jnp.max(s, axis=1, keepdims=True)
        e = jnp.exp2((s - top) * (FACTOR * math.log2(math.e)))
        inv = 1.0 / jnp.sum(e, axis=1, keepdims=True)
        mu = jnp.sum(e * ds, axis=1, keepdims=True) * inv
        t = (e * (ds - mu)).astype(BF)
        vd = recv[h, 2]
        both = jnp.dot(e.astype(BF), vd, preferred_element_type=F32)
        turn = jnp.dot(t, vd[:, :128], preferred_element_type=F32)
        o = both[:, :128] * inv
        do = (both[:, 128:] + turn * FACTOR) * inv
        return o.astype(BF), do.astype(BF)

    def swap(h, pair):
        two = pl.ds(pair * 2, 2)
        col = pl.ds(pl.multiple_of(x * GW + h * 128, 128), 128)
        k = 2 if pair == 1 else h // 2
        send(pb.at[h, two], ob.at[two, y, :, :, col], pre_send, pre_recv.at[k], partner)

    def swapped(k):
        width = (256, 128, 384)[k]
        wait(ob.at[pl.ds(0, 2), 0, :, :, pl.ds(0, width)], pre_recv.at[k])

    def attention(h):
        own_col = pl.ds(pl.multiple_of(x * GW + h * 128, 128), 128)

        def for_partner(j, _):
            o, do = attend(h, (1 - y) * 2 + j)
            for i in (0, 1):
                pb[h, j * 2 + i, 0] = o[i * 128 : (i + 1) * 128]
                pb[h, j * 2 + i, 1] = do[i * 128 : (i + 1) * 128]
            return 0

        def for_self(j, _):
            o, do = attend(h, y * 2 + j)
            for i in (0, 1):
                ob[j * 2 + i, y, 0, :, own_col] = o[i * 128 : (i + 1) * 128]
                ob[j * 2 + i, y, 1, :, own_col] = do[i * 128 : (i + 1) * 128]
            return 0

        if h < 2:
            lax.fori_loop(0, 2, for_partner, 0)
            swap(h, 0)
        else:
            for_partner(0, 0)
            for earlier, pair in ((2, 0), (0, 1), (1, 1)):
                swap(earlier, pair)
            for_partner(1, 0)
            swap(2, 1)
        lax.fori_loop(0, 2, for_self, 0)

    def unit(p, part, which, from_x):
        rb, first, rows = PIECES[p]
        skip, width = PARTS[part]
        col = pl.ds(pl.multiple_of(from_x * GW + skip, 128), width)
        group = y if which == 0 else 1 - y
        k = p * 4 + part * 2 + which if p < 2 else 4 + p * 2 + which
        return ob.at[rb, group, :, pl.ds(first, rows), col], k

    def x_unit(p, part, which):
        src, k = unit(p, part, which, x)
        send(src, src, x_send, x_recv.at[k], right)
        send(src, src, x_send, x_recv.at[k], left)

    def forward(p, part, which):
        rb, first, rows = PIECES[p]
        src, k = unit(p, part, which, xl)
        two = ob.at[rb, :, :, pl.ds(first, rows), pl.ds(0, PARTS[part][1])]
        wait(two, x_recv.at[k])
        send(src.at[0], src.at[0], x_send, f_recv.at[p], right)
        src, k = unit(p, part, which, xr)
        send(src.at[1], src.at[1], x_send, f_recv.at[p], left)

    def all_unit(p, which):
        x_unit(p, 2, which)
        src, _ = unit(p, 2, which, x)
        send(src, src, x_send, f_recv.at[p], {"dp": dp, "head": y * X + lax.rem(x + 2, X)})

    def arrived(p):
        rb, first, rows = PIECES[p]
        if p == ALL:
            for which in (0, 1):
                _, k = unit(p, 2, which, x)
                wait(ob.at[rb, :, :, pl.ds(first, rows), pl.ds(0, GW)], x_recv.at[k])
        wait(ob.at[rb, :, :, pl.ds(first, rows), pl.ds(0, GW)], f_recv.at[p])

    wait(shard(3).at[z, c], wy_recv.at[3])
    shard_along_z(3)

    wait(recv.at[0, 2], v_recv.at[0])
    wait(recv.at[1, 2], v_recv.at[1])
    sends_q(1)
    sends_v(2)

    shard_to_core(0)
    wait(gall.at[:, z, c], g_recv.at[0])
    for d in (1, 3, 2):
        send(gall.at[:, z, c], gall.at[:, z, c], g_send.at[1], g_recv.at[1], z_peer(d))

    wait(recv.at[0, pl.ds(0, 2)], q_recv.at[0])
    sends_q(2)
    src = shard(0).at[z, c]
    send(src, src, wy_send, wy_recv.at[1], y_chip(1))
    attention(0)

    shard_to_core(3)
    wait(recv.at[1, pl.ds(0, 2)], q_recv.at[1])
    attention(1)
    x_unit(0, 0, 0)
    x_unit(1, 0, 0)

    wait(gall.at[:, pl.ds(0, 3), c], g_recv.at[1])
    send(gall.at[:, :, c], gall.at[:, :, c], g_send.at[2], g_recv.at[2], other_core)

    wait(recv.at[2], q_recv.at[2])
    attention(2)
    x_unit(0, 1, 0)
    x_unit(1, 1, 0)
    wait(shard(1).at[z, c], wy_recv.at[1])
    shard_along_z(1)
    src = shard(1).at[z, c]
    send(src, src, wy_send, wy_recv.at[2], y_chip(3))
    forward(0, 0, 0)
    forward(1, 0, 0)
    x_unit(2, 2, 0)
    swapped(0)
    x_unit(0, 0, 1)
    wait(shard(2).at[z, c], wy_recv.at[2])
    shard_along_z(2)
    forward(0, 1, 0)
    swapped(1)
    x_unit(0, 1, 1)
    x_unit(1, 0, 1)
    forward(0, 0, 1)
    shard_to_core(1)
    forward(1, 1, 0)
    x_unit(1, 1, 1)
    forward(0, 1, 1)
    forward(1, 0, 1)
    forward(1, 1, 1)
    swapped(2)
    x_unit(2, 2, 1)
    x_unit(3, 2, 0)

    wait(gall.at[:, :, 1 - c], g_recv.at[2])
    moment = time[dp].astype(F32)
    speed = ttan[dp]
    freq = const[1:2, :]
    cos_t, sin_t = jnp.cos(moment * freq), jnp.sin(moment * freq)
    row = lax.broadcasted_iota(jnp.int32, (16, 256), 0)
    emb = jnp.concatenate([cos_t, sin_t], axis=1)
    demb = jnp.concatenate([-freq * sin_t, freq * cos_t], axis=1) * speed
    embs = jnp.where(row == 0, emb, jnp.where(row == 1, demb, 0.0)).astype(BF)
    gates = jnp.dot(embs, gall[...].reshape(256, COLS), preferred_element_type=F32)
    gate, dgate = gates[0:1], gates[1:2]

    wait(wall.at[1 - y, :, :, 1 - c], wc_recv.at[1])
    wait(resv, res_sem)

    def finish(rows, attn, dattn):
        out[rows, :] = (resv[0, rows, :].astype(F32) + gate * attn).astype(BF)
        otan[rows, :] = (resv[1, rows, :].astype(F32) + dgate * attn + gate * dattn).astype(BF)

    def project(rb, first, rows, yl):
        total = None
        for gy in (0, 1):
            term = jnp.dot(
                ob[rb, gy, :, first : first + rows, :].reshape(2 * rows, 1536),
                wall[yl, gy].reshape(1536, COLS),
                preferred_element_type=F32,
            )
            total = term if total is None else total + term
        return total

    def own_block(rb):
        total = project(rb, 0, ROWS, y)
        start = pl.multiple_of(y * HALF + rb * ROWS, ROWS)
        finish(pl.ds(start, ROWS), total[:ROWS], total[ROWS:])

    for p, (rb, first, rows) in enumerate(PIECES):
        arrived(p)
        total = project(rb, first, rows, 1 - y)
        both = pl.ds(0, 2 * rows)
        po[p, both] = total.astype(BF)
        send(po.at[p, both], pr.at[p, both], y_send, y_recv.at[p], partner)
        if p == 0:
            forward(2, 2, 0)
            x_unit(3, 2, 1)
            shard_to_core(2)
        elif p == 1:
            forward(2, 2, 1)
            x_unit(4, 2, 0)
            forward(3, 2, 0)
            x_unit(4, 2, 1)
            wait(wall.at[y, :, :, 1 - c], wc_recv.at[0])
            own_block(0)
        elif p == 2:
            forward(3, 2, 1)
            x_unit(6, 2, 0)
            forward(4, 2, 0)
            x_unit(6, 2, 1)
            forward(4, 2, 1)
            all_unit(ALL, 0)
            own_block(1)
        elif p == 3:
            all_unit(ALL, 1)
            own_block(2)
            forward(6, 2, 0)
            forward(6, 2, 1)
        elif p == 6:
            own_block(3)

    wait(sv.at[:, pl.ds(0, 7)], v_send)
    wait(sq.at[:, pl.ds(0, 7)], q_send)
    wait(pb, pre_send)
    wait(wall.at[0, 0, pl.ds(0, 3), 0], wy_send)
    wait(wall.at[:, :, pl.ds(0, 3), 0], wz_send)
    wait(wall.at[:, :, :, 0], wc_send)
    wait(gall.at[0, 0, 0], g_send.at[0])
    wait(gall.at[:, pl.ds(0, 3), 0], g_send.at[1])
    wait(gall.at[:, :, 0], g_send.at[2])
    wait(ob.at[:, :, :, :, pl.ds(0, 3 * GW)], x_send)

    for p, (rb, first, rows) in enumerate(PIECES):
        wait(pr.at[p, pl.ds(0, 2 * rows)], y_recv.at[p])
        start = pl.multiple_of((1 - y) * HALF + rb * 128 + first, 32)
        finish(
            pl.ds(start, rows),
            pr[p, 0:rows].astype(F32),
            pr[p, rows : 2 * rows].astype(F32),
        )
    wait(po.at[pl.ds(0, 4)], y_send)


def copy_kernel(a, b, out_a, out_b, sem):
    copies = []
    for i in range(2):
        rows = pl.ds(i * (SEQ // 2), SEQ // 2)
        for j, (src, dst) in enumerate(((a, out_a), (b, out_b))):
            copies.append(pltpu.make_async_copy(src.at[rows], dst.at[rows], sem.at[j, i]))
    for copy in copies:
        copy.start()
    for copy in copies:
        copy.wait()


def per_device(
    projections,
    projection_tangent,
    position_ids,
    norm_gain,
    out_weight,
    timestep,
    time_tangent,
    gate_weight,
    residual,
    residual_tangent,
):
    anywhere = pl.BlockSpec(memory_space=pl.ANY)
    dma = pltpu.SemaphoreType.DMA
    shape = jax.ShapeDtypeStruct((SEQ, COLS), BF)
    results = pl.pallas_call(
        kernel,
        out_shape=(pltpu.VMEM((SEQ, COLS), BF),) * 2,
        in_specs=[pl.BlockSpec(memory_space=pltpu.HBM)] * 11,
        out_specs=(pl.BlockSpec(memory_space=pltpu.VMEM),) * 2,
        scratch_shapes=[
            pltpu.VMEM((3, ROWS), jnp.int32),
            pltpu.VMEM((2, ATT_W), F32),
            pltpu.SMEM((16,), jnp.int32),
            pltpu.SMEM((16,), F32),
            pltpu.VMEM((8, 128), F32),
            pltpu.VMEM((2, 2, ROWS, ATT_W), BF),
            pltpu.VMEM((3, 8, ROWS, 256), BF),
            pltpu.VMEM((3, 8, 2, ROWS, 256), BF),
            pltpu.VMEM((3, 3, SEQ, 256), BF),
            pltpu.VMEM((4, 2, 2, ROWS, 1536), BF),
            pltpu.VMEM((3, 4, 2, ROWS, 128), BF),
            pltpu.VMEM((2, 2, 4, 2, 192, COLS), BF),
            pltpu.VMEM((2, 4, 2, 16, COLS), BF),
            pltpu.VMEM((2, SEQ, COLS), BF),
            pltpu.VMEM((7, 256, COLS), BF),
            pltpu.VMEM((7, 256, COLS), BF),
            dma((5,)),
            dma((2,)),
            dma,
            dma,
            dma((2,)),
            dma,
            dma((3,)),
            dma,
            dma((3,)),
            dma,
            dma((4,)),
            dma,
            dma((4,)),
            dma,
            dma((2,)),
            dma((3,)),
            dma((3,)),
            dma,
            dma((18,)),
            dma((7,)),
            dma,
            dma((7,)),
        ],
        compiler_params=pltpu.CompilerParams(
            collective_id=0, has_side_effects=True, vmem_limit_bytes=56 * 2**20
        ),
    )(
        projections,
        projection_tangent,
        position_ids.T,
        norm_gain,
        out_weight,
        timestep,
        time_tangent,
        gate_weight,
        residual,
        residual_tangent,
        jnp.asarray(CONST),
    )
    return pl.pallas_call(
        copy_kernel,
        out_shape=(shape, shape),
        in_specs=[anywhere, anywhere],
        out_specs=(anywhere, anywhere),
        scratch_shapes=[dma((2, 2))],
        compiler_params=pltpu.CompilerParams(vmem_limit_bytes=8 * 2**20),
    )(*results)


def solution(mesh):
    placed = (
        P(None, ("dp", "head"), None),
        P(None, ("dp", "head"), None),
        P(("dp", "head"), None),
        P(),
        P("dp", "head"),
        P(),
        P(),
        P("dp", None),
        P("dp", "head"),
        P("dp", "head"),
    )
    return jax.shard_map(
        per_device,
        mesh=mesh,
        in_specs=placed,
        out_specs=(P("dp", "head"), P("dp", "head")),
        check_vma=False,
    )
```

```python
import math

import jax
import jax.numpy as jnp
import numpy as np
from jax import lax
from jax.experimental import pallas as pl
from jax.experimental.pallas import tpu as pltpu
from jax.sharding import PartitionSpec as P

HEAD_DIM = 128
ATT_W = 3072
EPSILON = 1e-06
MESH = pl.DeviceIdType.MESH
BF = jnp.bfloat16
F32 = jnp.float32

X = 4
ROWS = 128
SEQ = 1024
HALF = 512
GW = 384
COLS = 640
FACTOR = HEAD_DIM ** (-0.5)

PIECES = (
    (0, 0, 128),
    (1, 0, 128),
    (2, 0, 64),
    (2, 64, 64),
    (3, 0, 64),
    (3, 64, 32),
    (3, 96, 32),
)
ALL = 5
PARTS = ((0, 256), (256, 128), (0, 384))

ORDER = ((1, 0), (0, 1), (0, 3), (1, 2), (0, 2), (1, 1), (1, 3))


def constants():
    pair_count = HEAD_DIM // 2
    height_pairs = HEAD_DIM // 6
    time_pairs = pair_count - 2 * height_pairs
    j = np.arange(pair_count)
    local = np.where(
        j < time_pairs,
        j,
        np.where(j < time_pairs + height_pairs, j - time_pairs, j - time_pairs - height_pairs),
    )
    span = np.where(j < time_pairs, time_pairs, height_pairs)
    rope = np.repeat(np.power(10000.0, -local / span), 2)
    clock = np.power(10000.0, -np.arange(128) / 128)
    rows = np.zeros((8, 128), np.float32)
    rows[0] = rope
    rows[1] = clock
    return rows, 2 * time_pairs, 2 * (time_pairs + height_pairs)


CONST, LANE_ROW, LANE_COL = constants()


def nt_dot(a, b):
    return lax.dot_general(a, b, (((1,), (1,)), ((), ())), preferred_element_type=F32)


def kernel(
    proj,
    tan,
    pos_hbm,
    gain_hbm,
    wout,
    time_hbm,
    ttan_hbm,
    wgate,
    res,
    rtan,
    const_hbm,
    out,
    otan,
    pos,
    gain,
    time,
    ttan,
    const,
    raw,
    sv,
    sq,
    recv,
    ob,
    pb,
    wall,
    gall,
    resv,
    po,
    pr,
    small_sem,
    load_sem,
    res_sem,
    v_send,
    v_recv,
    q_send,
    q_recv,
    pre_send,
    pre_recv,
    wy_send,
    wy_recv,
    wz_send,
    wz_recv,
    wc_send,
    wc_recv,
    g_send,
    g_recv,
    x_send,
    x_recv,
    f_recv,
    y_send,
    y_recv,
):
    dp = lax.axis_index("dp")
    head = lax.axis_index("head")
    y, x = head // X, lax.rem(head, X)
    yh, z, c = dp // 8, lax.rem(dp // 2, 4), lax.rem(dp, 2)
    partner = {"dp": dp, "head": (1 - y) * X + x}
    right = {"dp": dp, "head": y * X + lax.rem(x + 1, X)}
    left = {"dp": dp, "head": y * X + lax.rem(x + 3, X)}
    xl, xr = lax.rem(x + 3, X), lax.rem(x + 1, X)
    other_core = {"dp": dp + 1 - 2 * c, "head": head}

    def z_peer(d):
        return {"dp": yh * 8 + lax.rem(z + d, 4) * 2 + c, "head": head}

    def send(src, dst, ssem, rsem, to):
        pltpu.make_async_remote_copy(
            src_ref=src,
            dst_ref=dst,
            send_sem=ssem,
            recv_sem=rsem,
            device_id=to,
            device_id_type=MESH,
        ).start()

    def local(src, dst, sem):
        pltpu.make_async_copy(src, dst, sem).start()

    def wait(ref, sem):
        pltpu.make_async_copy(ref, ref, sem).wait()

    def sends_v(h):
        for dy, dx in ORDER:
            g = lax.rem(y + dy, 2) * X + lax.rem(x + dx, X)
            to = {"dp": dp, "head": g}
            send(sv.at[h, g], recv.at[h, 2, mine], v_send, (v_recv if h < 2 else q_recv).at[h], to)
        local(sv.at[h, head], recv.at[h, 2, mine], (v_recv if h < 2 else q_recv).at[h])

    def send_q(h, g):
        to = {"dp": dp, "head": g}
        send(sq.at[h, g], recv.at[h, pl.ds(0, 2), mine], q_send, q_recv.at[h], to)

    def sends_q(h):
        for dy, dx in ORDER:
            send_q(h, lax.rem(y + dy, 2) * X + lax.rem(x + dx, X))
        local(sq.at[h, head], recv.at[h, pl.ds(0, 2), mine], q_recv.at[h])

    def shard(s):
        return wall.at[y if s in (0, 2) else 1 - y, yh if s in (0, 1) else 1 - yh]

    def y_chip(s):
        row = yh if s in (0, 1) else 1 - yh
        return {
            "dp": row * 8 + z * 2 + c,
            "head": (y if s in (0, 2) else 1 - y) * X + x,
        }

    def shard_along_z(s):
        for d in (1, 3, 2):
            src = shard(s).at[z, c]
            send(src, src, wz_send, wz_recv.at[s], z_peer(d))

    def shard_to_core(s):
        wait(shard(s).at[pl.ds(0, 3), c], wz_recv.at[s])
        src = shard(s).at[:, c]
        send(src, src, wc_send, wc_recv.at[s % 2], other_core)

    mine = pl.ds(pl.multiple_of(head * ROWS, ROWS), ROWS)
    gate_cols = wgate.at[:, pl.ds(pl.multiple_of(head * COLS, 128), COLS)]

    barrier = pltpu.get_barrier_semaphore()
    for dy, dx in ORDER:
        to = {"dp": dp, "head": lax.rem(y + dy, 2) * X + lax.rem(x + dx, X)}
        pl.semaphore_signal(barrier, inc=1, device_id=to, device_id_type=MESH)
    for to in (z_peer(1), z_peer(2), z_peer(3), other_core, y_chip(2), y_chip(3)):
        pl.semaphore_signal(barrier, inc=1, device_id=to, device_id_type=MESH)

    for h in range(3):

        def load_v(g, _, h=h):
            col = pl.ds(pl.multiple_of(g * GW + h * 128, 128), 128)
            local(proj.at[2, :, col], sv.at[h, g, :, pl.ds(0, 128)], load_sem.at[0])
            local(tan.at[2, :, col], sv.at[h, g, :, pl.ds(128, 128)], load_sem.at[0])
            return 0

        lax.fori_loop(0, 8, load_v, 0)
    local(wout, shard(0).at[z, c], wy_recv.at[0])
    small = ((pos_hbm, pos), (gain_hbm, gain), (time_hbm, time), (ttan_hbm, ttan), (const_hbm, const))
    for i, (src, dst) in enumerate(small):
        local(src, dst, small_sem.at[i])
    local(proj.at[pl.ds(0, 2)], raw.at[0], load_sem.at[1])
    local(tan.at[pl.ds(0, 2)], raw.at[1], load_sem.at[1])
    local(gate_cols, gall.at[yh, z, c], g_recv.at[0])
    local(res, resv.at[0], res_sem)
    local(rtan, resv.at[1], res_sem)

    pl.semaphore_wait(barrier, 13)

    wait(shard(0).at[z, c], wy_recv.at[0])
    src = shard(0).at[z, c]
    send(src, src, wy_send, wy_recv.at[3], y_chip(3))
    shard_along_z(0)
    wait(sv, load_sem.at[0])
    sends_v(0)
    sends_v(1)
    send(gate_cols, gall.at[yh, z, c], g_send.at[0], g_recv.at[0], y_chip(2))

    for i, (_, dst) in enumerate(small):
        wait(dst, small_sem.at[i])

    line = lax.broadcasted_iota(jnp.int32, (128, ROWS), 0)
    ids = pos[...].astype(F32)
    chosen = jnp.where(
        line < LANE_ROW, ids[0:1, :], jnp.where(line < LANE_COL, ids[1:2, :], ids[2:3, :])
    )
    angle = jnp.transpose(chosen) * const[0:1, :]
    lane = lax.broadcasted_iota(jnp.int32, (ROWS, 128), 1)
    even = lax.rem(lane, 2) == 0
    cosine, sine = jnp.cos(angle), jnp.sin(angle)
    sine = jnp.where(even, -sine, sine)

    def rotate(m):
        swapped = jnp.where(even, pltpu.roll(m, 127, 1), pltpu.roll(m, 1, 1))
        return (m * cosine + swapped * sine).astype(BF)

    wait(raw, load_sem.at[1])
    stats = []
    for a in (0, 1):

        def add(i, carry, a=a):
            square, cross = carry
            col = pl.ds(pl.multiple_of(i * 128, 128), 128)
            q = raw[0, a, :, col].astype(F32)
            dq = raw[1, a, :, col].astype(F32)
            return square + q * q, cross + q * dq

        zero = jnp.zeros((ROWS, 128), F32)
        square, cross = lax.fori_loop(0, ATT_W // 128, add, (zero, zero))
        r = lax.rsqrt(jnp.sum(square, axis=1, keepdims=True) / ATT_W + EPSILON)
        cr = jnp.sum(cross, axis=1, keepdims=True) / ATT_W
        stats.append((r, r * r * r * cr))

    for h in range(3):

        def prepare(i, _, h=h):
            g = lax.rem(y + i // X, 2) * X + lax.rem(x + i, X)
            col = pl.ds(pl.multiple_of(g * GW + h * 128, 128), 128)
            for a in (0, 1):
                r, rc = stats[a]
                q = raw[0, a, :, col].astype(F32)
                dq = raw[1, a, :, col].astype(F32)
                gn = gain[a : a + 1, col]
                n = rotate(q * r * gn)
                dn = rotate(gn * (dq * r - q * rc))
                sq[h, g, a, :, 0:128] = dn if a == 0 else n
                sq[h, g, a, :, 128:256] = n if a == 0 else dn

            if h == 0:

                @pl.when(i > 0)
                def _():
                    send_q(h, g)

            return 0

        lax.fori_loop(0, 8, prepare, 0)
        if h == 0:
            local(sq.at[h, head], recv.at[h, pl.ds(0, 2), mine], q_recv.at[h])

    def attend(h, block):
        rows = pl.ds(pl.multiple_of(block * 256, 256), 256)
        qd = recv[h, 0, rows, :]
        kd = recv[h, 1]
        s = nt_dot(qd[:, 128:], kd[:, :128])
        ds = nt_dot(qd, kd)
        top = jnp.max(s, axis=1, keepdims=True)
        e = jnp.exp2((s - top) * (FACTOR * math.log2(math.e)))
        inv = 1.0 / jnp.sum(e, axis=1, keepdims=True)
        mu = jnp.sum(e * ds, axis=1, keepdims=True) * inv
        t = (e * (ds - mu)).astype(BF)
        vd = recv[h, 2]
        both = jnp.dot(e.astype(BF), vd, preferred_element_type=F32)
        turn = jnp.dot(t, vd[:, :128], preferred_element_type=F32)
        o = both[:, :128] * inv
        do = (both[:, 128:] + turn * FACTOR) * inv
        return o.astype(BF), do.astype(BF)

    def swap(h, pair):
        two = pl.ds(pair * 2, 2)
        col = pl.ds(pl.multiple_of(x * GW + h * 128, 128), 128)
        k = 2 if pair == 1 else h // 2
        send(pb.at[h, two], ob.at[two, y, :, :, col], pre_send, pre_recv.at[k], partner)

    def swapped(k):
        width = (256, 128, 384)[k]
        wait(ob.at[pl.ds(0, 2), 0, :, :, pl.ds(0, width)], pre_recv.at[k])

    def attention(h):
        own_col = pl.ds(pl.multiple_of(x * GW + h * 128, 128), 128)

        def for_partner(j, _):
            o, do = attend(h, (1 - y) * 2 + j)
            for i in (0, 1):
                pb[h, j * 2 + i, 0] = o[i * 128 : (i + 1) * 128]
                pb[h, j * 2 + i, 1] = do[i * 128 : (i + 1) * 128]
            return 0

        def for_self(j, _):
            o, do = attend(h, y * 2 + j)
            for i in (0, 1):
                ob[j * 2 + i, y, 0, :, own_col] = o[i * 128 : (i + 1) * 128]
                ob[j * 2 + i, y, 1, :, own_col] = do[i * 128 : (i + 1) * 128]
            return 0

        if h < 2:
            lax.fori_loop(0, 2, for_partner, 0)
            swap(h, 0)
        else:
            for_partner(0, 0)
            for earlier, pair in ((2, 0), (0, 1), (1, 1)):
                swap(earlier, pair)
            for_partner(1, 0)
            swap(2, 1)
        lax.fori_loop(0, 2, for_self, 0)

    def unit(p, part, which, from_x):
        rb, first, rows = PIECES[p]
        skip, width = PARTS[part]
        col = pl.ds(pl.multiple_of(from_x * GW + skip, 128), width)
        group = y if which == 0 else 1 - y
        k = p * 4 + part * 2 + which if p < 2 else 4 + p * 2 + which
        return ob.at[rb, group, :, pl.ds(first, rows), col], k

    def x_unit(p, part, which):
        src, k = unit(p, part, which, x)
        send(src, src, x_send, x_recv.at[k], right)
        send(src, src, x_send, x_recv.at[k], left)

    def forward(p, part, which):
        rb, first, rows = PIECES[p]
        src, k = unit(p, part, which, xl)
        two = ob.at[rb, :, :, pl.ds(first, rows), pl.ds(0, PARTS[part][1])]
        wait(two, x_recv.at[k])
        send(src.at[0], src.at[0], x_send, f_recv.at[p], right)
        src, k = unit(p, part, which, xr)
        send(src.at[1], src.at[1], x_send, f_recv.at[p], left)

    def all_unit(p, which):
        x_unit(p, 2, which)
        src, _ = unit(p, 2, which, x)
        send(src, src, x_send, f_recv.at[p], {"dp": dp, "head": y * X + lax.rem(x + 2, X)})

    def arrived(p):
        rb, first, rows = PIECES[p]
        wait(ob.at[rb, :, :, pl.ds(first, rows), pl.ds(0, GW)], f_recv.at[p])

    def arrived_near(p):
        rb, first, rows = PIECES[p]
        for which in (0, 1):
            _, k = unit(p, 2, which, x)
            wait(ob.at[rb, :, :, pl.ds(first, rows), pl.ds(0, GW)], x_recv.at[k])

    wait(shard(3).at[z, c], wy_recv.at[3])
    shard_along_z(3)

    wait(recv.at[0, 2], v_recv.at[0])
    wait(recv.at[1, 2], v_recv.at[1])
    sends_q(1)
    sends_v(2)

    shard_to_core(0)
    wait(gall.at[:, z, c], g_recv.at[0])
    for d in (1, 3, 2):
        send(gall.at[:, z, c], gall.at[:, z, c], g_send.at[1], g_recv.at[1], z_peer(d))

    wait(recv.at[0, pl.ds(0, 2)], q_recv.at[0])
    sends_q(2)
    src = shard(0).at[z, c]
    send(src, src, wy_send, wy_recv.at[1], y_chip(1))
    attention(0)

    shard_to_core(3)
    wait(recv.at[1, pl.ds(0, 2)], q_recv.at[1])
    attention(1)
    x_unit(0, 0, 0)
    x_unit(1, 0, 0)

    wait(gall.at[:, pl.ds(0, 3), c], g_recv.at[1])
    send(gall.at[:, :, c], gall.at[:, :, c], g_send.at[2], g_recv.at[2], other_core)

    wait(recv.at[2], q_recv.at[2])
    attention(2)
    x_unit(0, 1, 0)
    x_unit(1, 1, 0)
    wait(shard(1).at[z, c], wy_recv.at[1])
    shard_along_z(1)
    src = shard(1).at[z, c]
    send(src, src, wy_send, wy_recv.at[2], y_chip(3))
    forward(0, 0, 0)
    forward(1, 0, 0)
    x_unit(2, 2, 0)
    swapped(0)
    x_unit(0, 0, 1)
    wait(shard(2).at[z, c], wy_recv.at[2])
    shard_along_z(2)
    forward(0, 1, 0)
    swapped(1)
    x_unit(0, 1, 1)
    x_unit(1, 0, 1)
    forward(0, 0, 1)
    shard_to_core(1)
    forward(1, 1, 0)
    x_unit(1, 1, 1)
    forward(0, 1, 1)
    forward(1, 0, 1)
    forward(1, 1, 1)
    swapped(2)
    x_unit(2, 2, 1)
    x_unit(3, 2, 0)

    wait(gall.at[:, :, 1 - c], g_recv.at[2])
    moment = time[dp].astype(F32)
    speed = ttan[dp]
    freq = const[1:2, :]
    cos_t, sin_t = jnp.cos(moment * freq), jnp.sin(moment * freq)
    row = lax.broadcasted_iota(jnp.int32, (16, 256), 0)
    emb = jnp.concatenate([cos_t, sin_t], axis=1)
    demb = jnp.concatenate([-freq * sin_t, freq * cos_t], axis=1) * speed
    embs = jnp.where(row == 0, emb, jnp.where(row == 1, demb, 0.0)).astype(BF)
    gates = jnp.dot(embs, gall[...].reshape(256, COLS), preferred_element_type=F32)
    gate, dgate = gates[0:1], gates[1:2]

    wait(wall.at[1 - y, :, :, 1 - c], wc_recv.at[1])
    wait(resv, res_sem)

    def finish(rows, attn, dattn):
        out[rows, :] = (resv[0, rows, :].astype(F32) + gate * attn).astype(BF)
        otan[rows, :] = (resv[1, rows, :].astype(F32) + dgate * attn + gate * dattn).astype(BF)

    def project(rb, first, rows, yl):
        total = None
        for gy in (0, 1):
            term = jnp.dot(
                ob[rb, gy, :, first : first + rows, :].reshape(2 * rows, 1536),
                wall[yl, gy].reshape(1536, COLS),
                preferred_element_type=F32,
            )
            total = term if total is None else total + term
        return total

    def project_from(rb, first, rows, yl, offsets):
        total = None
        for gy in (0, 1):
            for offset in offsets:
                at = lax.rem(x + offset, X)
                col = pl.ds(pl.multiple_of(at * GW, 128), GW)
                term = jnp.dot(
                    ob[rb, gy, :, first : first + rows, col].reshape(2 * rows, GW),
                    wall[yl, gy, at].reshape(GW, COLS),
                    preferred_element_type=F32,
                )
                total = term if total is None else total + term
        return total

    def own_block(rb):
        total = project(rb, 0, ROWS, y)
        start = pl.multiple_of(y * HALF + rb * ROWS, ROWS)
        finish(pl.ds(start, ROWS), total[:ROWS], total[ROWS:])

    for p, (rb, first, rows) in enumerate(PIECES):
        if p == ALL:
            arrived_near(p)
            near = project_from(rb, first, 2 * rows, 1 - y, (0, 1, 3))
        arrived(p)
        if p < ALL:
            total = project(rb, first, rows, 1 - y)
        else:
            at = (p - ALL) * rows
            total = jnp.concatenate([near[at : at + rows], near[2 * rows + at : 3 * rows + at]])
            total = total + project_from(rb, first, rows, 1 - y, (2,))
        both = pl.ds(0, 2 * rows)
        po[p, both] = total.astype(BF)
        send(po.at[p, both], pr.at[p, both], y_send, y_recv.at[p], partner)
        if p == 0:
            forward(2, 2, 0)
            x_unit(3, 2, 1)
            shard_to_core(2)
        elif p == 1:
            forward(2, 2, 1)
            x_unit(4, 2, 0)
            forward(3, 2, 0)
            x_unit(4, 2, 1)
            wait(wall.at[y, :, :, 1 - c], wc_recv.at[0])
            own_block(0)
        elif p == 2:
            forward(3, 2, 1)
            x_unit(6, 2, 0)
            forward(4, 2, 0)
            x_unit(6, 2, 1)
            forward(4, 2, 1)
            all_unit(ALL, 0)
            all_unit(ALL, 1)
            own_block(1)
        elif p == 3:
            own_block(2)
            forward(6, 2, 0)
            forward(6, 2, 1)
        elif p == 6:
            own_block(3)

    wait(sv.at[:, pl.ds(0, 7)], v_send)
    wait(sq.at[:, pl.ds(0, 7)], q_send)
    wait(pb, pre_send)
    wait(wall.at[0, 0, pl.ds(0, 3), 0], wy_send)
    wait(wall.at[:, :, pl.ds(0, 3), 0], wz_send)
    wait(wall.at[:, :, :, 0], wc_send)
    wait(gall.at[0, 0, 0], g_send.at[0])
    wait(gall.at[:, pl.ds(0, 3), 0], g_send.at[1])
    wait(gall.at[:, :, 0], g_send.at[2])
    wait(ob.at[:, :, :, :, pl.ds(0, 3 * GW)], x_send)

    for p, (rb, first, rows) in enumerate(PIECES):
        wait(pr.at[p, pl.ds(0, 2 * rows)], y_recv.at[p])
        start = pl.multiple_of((1 - y) * HALF + rb * 128 + first, 32)
        finish(
            pl.ds(start, rows),
            pr[p, 0:rows].astype(F32),
            pr[p, rows : 2 * rows].astype(F32),
        )
    wait(po.at[pl.ds(0, 4)], y_send)


def copy_kernel(a, b, out_a, out_b, sem):
    copies = []
    for i in range(1):
        rows = pl.ds(i * (SEQ // 1), SEQ // 1)
        for j, (src, dst) in enumerate(((a, out_a), (b, out_b))):
            copies.append(pltpu.make_async_copy(src.at[rows], dst.at[rows], sem.at[j, i]))
    for copy in copies:
        copy.start()
    for copy in copies:
        copy.wait()


def per_device(
    projections,
    projection_tangent,
    position_ids,
    norm_gain,
    out_weight,
    timestep,
    time_tangent,
    gate_weight,
    residual,
    residual_tangent,
):
    anywhere = pl.BlockSpec(memory_space=pl.ANY)
    dma = pltpu.SemaphoreType.DMA
    shape = jax.ShapeDtypeStruct((SEQ, COLS), BF)
    results = pl.pallas_call(
        kernel,
        out_shape=(pltpu.VMEM((SEQ, COLS), BF),) * 2,
        in_specs=[pl.BlockSpec(memory_space=pltpu.HBM)] * 11,
        out_specs=(pl.BlockSpec(memory_space=pltpu.VMEM),) * 2,
        scratch_shapes=[
            pltpu.VMEM((3, ROWS), jnp.int32),
            pltpu.VMEM((2, ATT_W), F32),
            pltpu.SMEM((16,), jnp.int32),
            pltpu.SMEM((16,), F32),
            pltpu.VMEM((8, 128), F32),
            pltpu.VMEM((2, 2, ROWS, ATT_W), BF),
            pltpu.VMEM((3, 8, ROWS, 256), BF),
            pltpu.VMEM((3, 8, 2, ROWS, 256), BF),
            pltpu.VMEM((3, 3, SEQ, 256), BF),
            pltpu.VMEM((4, 2, 2, ROWS, 1536), BF),
            pltpu.VMEM((3, 4, 2, ROWS, 128), BF),
            pltpu.VMEM((2, 2, 4, 2, 192, COLS), BF),
            pltpu.VMEM((2, 4, 2, 16, COLS), BF),
            pltpu.VMEM((2, SEQ, COLS), BF),
            pltpu.VMEM((7, 256, COLS), BF),
            pltpu.VMEM((7, 256, COLS), BF),
            dma((5,)),
            dma((2,)),
            dma,
            dma,
            dma((2,)),
            dma,
            dma((3,)),
            dma,
            dma((3,)),
            dma,
            dma((4,)),
            dma,
            dma((4,)),
            dma,
            dma((2,)),
            dma((3,)),
            dma((3,)),
            dma,
            dma((18,)),
            dma((7,)),
            dma,
            dma((7,)),
        ],
        compiler_params=pltpu.CompilerParams(
            collective_id=0, has_side_effects=True, vmem_limit_bytes=56 * 2**20
        ),
    )(
        projections,
        projection_tangent,
        position_ids.T,
        norm_gain,
        out_weight,
        timestep,
        time_tangent,
        gate_weight,
        residual,
        residual_tangent,
        jnp.asarray(CONST),
    )
    return pl.pallas_call(
        copy_kernel,
        out_shape=(shape, shape),
        in_specs=[anywhere, anywhere],
        out_specs=(anywhere, anywhere),
        scratch_shapes=[dma((2, 1))],
        compiler_params=pltpu.CompilerParams(vmem_limit_bytes=8 * 2**20),
    )(*results)


def solution(mesh):
    placed = (
        P(None, ("dp", "head"), None),
        P(None, ("dp", "head"), None),
        P(("dp", "head"), None),
        P(),
        P("dp", "head"),
        P(),
        P(),
        P("dp", None),
        P("dp", "head"),
        P("dp", "head"),
    )
    return jax.shard_map(
        per_device,
        mesh=mesh,
        in_specs=placed,
        out_specs=(P("dp", "head"), P("dp", "head")),
        check_vma=False,
    )
```

```python
import math

import jax
import jax.numpy as jnp
import numpy as np
from jax import lax
from jax.experimental import pallas as pl
from jax.experimental.pallas import tpu as pltpu
from jax.sharding import PartitionSpec as P

HEAD_DIM = 128
ATT_W = 3072
EPSILON = 1e-06
MESH = pl.DeviceIdType.MESH
BF = jnp.bfloat16
F32 = jnp.float32

X = 4
ROWS = 128
SEQ = 1024
HALF = 512
GW = 384
COLS = 640
FACTOR = HEAD_DIM ** (-0.5)

PIECES = (
    (0, 0, 128),
    (1, 0, 128),
    (2, 0, 64),
    (2, 64, 64),
    (3, 0, 64),
    (3, 64, 32),
    (3, 96, 32),
)
ALL = 5
PARTS = ((0, 256), (256, 128), (0, 384))

ORDER = ((1, 0), (0, 1), (0, 3), (1, 2), (0, 2), (1, 1), (1, 3))


def constants():
    pair_count = HEAD_DIM // 2
    height_pairs = HEAD_DIM // 6
    time_pairs = pair_count - 2 * height_pairs
    j = np.arange(pair_count)
    local = np.where(
        j < time_pairs,
        j,
        np.where(j < time_pairs + height_pairs, j - time_pairs, j - time_pairs - height_pairs),
    )
    span = np.where(j < time_pairs, time_pairs, height_pairs)
    rope = np.repeat(np.power(10000.0, -local / span), 2)
    clock = np.power(10000.0, -np.arange(128) / 128)
    rows = np.zeros((8, 128), np.float32)
    rows[0] = rope
    rows[1] = clock
    return rows, 2 * time_pairs, 2 * (time_pairs + height_pairs)


CONST, LANE_ROW, LANE_COL = constants()


def nt_dot(a, b):
    return lax.dot_general(a, b, (((1,), (1,)), ((), ())), preferred_element_type=F32)


def kernel(
    proj,
    tan,
    pos_hbm,
    gain_hbm,
    wout,
    time_hbm,
    ttan_hbm,
    wgate,
    res,
    rtan,
    const_hbm,
    out,
    otan,
    pos,
    gain,
    time,
    ttan,
    const,
    raw,
    sv,
    sq,
    recv,
    ob,
    pb,
    wall,
    gall,
    resv,
    po,
    pr,
    small_sem,
    load_sem,
    res_sem,
    v_send,
    v_recv,
    q_send,
    q_recv,
    pre_send,
    pre_recv,
    wy_send,
    wy_recv,
    wz_send,
    wz_recv,
    wc_send,
    wc_recv,
    g_send,
    g_recv,
    x_send,
    x_recv,
    f_recv,
    y_send,
    y_recv,
):
    dp = lax.axis_index("dp")
    head = lax.axis_index("head")
    y, x = head // X, lax.rem(head, X)
    yh, z, c = dp // 8, lax.rem(dp // 2, 4), lax.rem(dp, 2)
    partner = {"dp": dp, "head": (1 - y) * X + x}
    right = {"dp": dp, "head": y * X + lax.rem(x + 1, X)}
    left = {"dp": dp, "head": y * X + lax.rem(x + 3, X)}
    xl, xr = lax.rem(x + 3, X), lax.rem(x + 1, X)
    other_core = {"dp": dp + 1 - 2 * c, "head": head}

    def z_peer(d):
        return {"dp": yh * 8 + lax.rem(z + d, 4) * 2 + c, "head": head}

    def send(src, dst, ssem, rsem, to):
        pltpu.make_async_remote_copy(
            src_ref=src,
            dst_ref=dst,
            send_sem=ssem,
            recv_sem=rsem,
            device_id=to,
            device_id_type=MESH,
        ).start()

    def local(src, dst, sem):
        pltpu.make_async_copy(src, dst, sem).start()

    def wait(ref, sem):
        pltpu.make_async_copy(ref, ref, sem).wait()

    def sends_v(h):
        for dy, dx in ORDER:
            g = lax.rem(y + dy, 2) * X + lax.rem(x + dx, X)
            to = {"dp": dp, "head": g}
            send(sv.at[h, g], recv.at[h, 2, mine], v_send, (v_recv if h < 2 else q_recv).at[h], to)
        local(sv.at[h, head], recv.at[h, 2, mine], (v_recv if h < 2 else q_recv).at[h])

    def send_q(h, g):
        to = {"dp": dp, "head": g}
        send(sq.at[h, g], recv.at[h, pl.ds(0, 2), mine], q_send, q_recv.at[h], to)

    def sends_q(h):
        for dy, dx in ORDER:
            send_q(h, lax.rem(y + dy, 2) * X + lax.rem(x + dx, X))
        local(sq.at[h, head], recv.at[h, pl.ds(0, 2), mine], q_recv.at[h])

    def shard(s):
        return wall.at[y if s in (0, 2) else 1 - y, yh if s in (0, 1) else 1 - yh]

    def y_chip(s):
        row = yh if s in (0, 1) else 1 - yh
        return {
            "dp": row * 8 + z * 2 + c,
            "head": (y if s in (0, 2) else 1 - y) * X + x,
        }

    def shard_along_z(s):
        for d in (1, 3, 2):
            src = shard(s).at[z, c]
            send(src, src, wz_send, wz_recv.at[s], z_peer(d))

    def shard_to_core(s):
        wait(shard(s).at[pl.ds(0, 3), c], wz_recv.at[s])
        src = shard(s).at[:, c]
        send(src, src, wc_send, wc_recv.at[s % 2], other_core)

    mine = pl.ds(pl.multiple_of(head * ROWS, ROWS), ROWS)
    gate_cols = wgate.at[:, pl.ds(pl.multiple_of(head * COLS, 128), COLS)]

    barrier = pltpu.get_barrier_semaphore()
    for dy, dx in ORDER:
        to = {"dp": dp, "head": lax.rem(y + dy, 2) * X + lax.rem(x + dx, X)}
        pl.semaphore_signal(barrier, inc=1, device_id=to, device_id_type=MESH)
    for to in (z_peer(1), z_peer(2), z_peer(3), other_core, y_chip(2), y_chip(3)):
        pl.semaphore_signal(barrier, inc=1, device_id=to, device_id_type=MESH)

    for h in range(3):

        def load_v(g, _, h=h):
            col = pl.ds(pl.multiple_of(g * GW + h * 128, 128), 128)
            local(proj.at[2, :, col], sv.at[h, g, :, pl.ds(0, 128)], load_sem.at[0])
            local(tan.at[2, :, col], sv.at[h, g, :, pl.ds(128, 128)], load_sem.at[0])
            return 0

        lax.fori_loop(0, 8, load_v, 0)
    local(wout, shard(0).at[z, c], wy_recv.at[0])
    small = ((pos_hbm, pos), (gain_hbm, gain), (time_hbm, time), (ttan_hbm, ttan), (const_hbm, const))
    for i, (src, dst) in enumerate(small):
        local(src, dst, small_sem.at[i])
    local(proj.at[pl.ds(0, 2)], raw.at[0], load_sem.at[1])
    local(tan.at[pl.ds(0, 2)], raw.at[1], load_sem.at[1])
    local(gate_cols, gall.at[yh, z, c], g_recv.at[0])
    local(res, resv.at[0], res_sem)
    local(rtan, resv.at[1], res_sem)

    pl.semaphore_wait(barrier, 13)

    wait(sv, load_sem.at[0])
    sends_v(0)
    sends_v(1)
    wait(shard(0).at[z, c], wy_recv.at[0])
    src = shard(0).at[z, c]
    send(src, src, wy_send, wy_recv.at[3], y_chip(3))
    shard_along_z(0)
    send(gate_cols, gall.at[yh, z, c], g_send.at[0], g_recv.at[0], y_chip(2))

    for i, (_, dst) in enumerate(small):
        wait(dst, small_sem.at[i])

    line = lax.broadcasted_iota(jnp.int32, (128, ROWS), 0)
    ids = pos[...].astype(F32)
    chosen = jnp.where(
        line < LANE_ROW, ids[0:1, :], jnp.where(line < LANE_COL, ids[1:2, :], ids[2:3, :])
    )
    angle = jnp.transpose(chosen) * const[0:1, :]
    lane = lax.broadcasted_iota(jnp.int32, (ROWS, 128), 1)
    even = lax.rem(lane, 2) == 0
    cosine, sine = jnp.cos(angle), jnp.sin(angle)
    sine = jnp.where(even, -sine, sine)

    def rotate(m):
        swapped = jnp.where(even, pltpu.roll(m, 127, 1), pltpu.roll(m, 1, 1))
        return (m * cosine + swapped * sine).astype(BF)

    wait(raw, load_sem.at[1])
    stats = []
    for a in (0, 1):

        def add(i, carry, a=a):
            square, cross = carry
            col = pl.ds(pl.multiple_of(i * 128, 128), 128)
            q = raw[0, a, :, col].astype(F32)
            dq = raw[1, a, :, col].astype(F32)
            return square + q * q, cross + q * dq

        zero = jnp.zeros((ROWS, 128), F32)
        square, cross = lax.fori_loop(0, ATT_W // 128, add, (zero, zero))
        r = lax.rsqrt(jnp.sum(square, axis=1, keepdims=True) / ATT_W + EPSILON)
        cr = jnp.sum(cross, axis=1, keepdims=True) / ATT_W
        stats.append((r, r * r * r * cr))

    for h in range(3):

        def prepare(i, _, h=h):
            g = lax.rem(y + i // X, 2) * X + lax.rem(x + i, X)
            col = pl.ds(pl.multiple_of(g * GW + h * 128, 128), 128)
            for a in (0, 1):
                r, rc = stats[a]
                q = raw[0, a, :, col].astype(F32)
                dq = raw[1, a, :, col].astype(F32)
                gn = gain[a : a + 1, col]
                n = rotate(q * r * gn)
                dn = rotate(gn * (dq * r - q * rc))
                sq[h, g, a, :, 0:128] = dn if a == 0 else n
                sq[h, g, a, :, 128:256] = n if a == 0 else dn

            if h == 0:

                @pl.when(i > 0)
                def _():
                    send_q(h, g)

            return 0

        lax.fori_loop(0, 8, prepare, 0)
        if h == 0:
            local(sq.at[h, head], recv.at[h, pl.ds(0, 2), mine], q_recv.at[h])

    def attend(h, block):
        rows = pl.ds(pl.multiple_of(block * 256, 256), 256)
        qd = recv[h, 0, rows, :]
        kd = recv[h, 1]
        s = nt_dot(qd[:, 128:], kd[:, :128])
        ds = nt_dot(qd, kd)
        top = jnp.max(s, axis=1, keepdims=True)
        e = jnp.exp2((s - top) * (FACTOR * math.log2(math.e)))
        inv = 1.0 / jnp.sum(e, axis=1, keepdims=True)
        mu = jnp.sum(e * ds, axis=1, keepdims=True) * inv
        t = (e * (ds - mu)).astype(BF)
        vd = recv[h, 2]
        both = jnp.dot(e.astype(BF), vd, preferred_element_type=F32)
        turn = jnp.dot(t, vd[:, :128], preferred_element_type=F32)
        o = both[:, :128] * inv
        do = (both[:, 128:] + turn * FACTOR) * inv
        return o.astype(BF), do.astype(BF)

    def swap(h, pair):
        two = pl.ds(pair * 2, 2)
        col = pl.ds(pl.multiple_of(x * GW + h * 128, 128), 128)
        k = 2 if pair == 1 else h // 2
        send(pb.at[h, two], ob.at[two, y, :, :, col], pre_send, pre_recv.at[k], partner)

    def swapped(k):
        width = (256, 128, 384)[k]
        wait(ob.at[pl.ds(0, 2), 0, :, :, pl.ds(0, width)], pre_recv.at[k])

    def attention(h):
        own_col = pl.ds(pl.multiple_of(x * GW + h * 128, 128), 128)

        def for_partner(j, _):
            o, do = attend(h, (1 - y) * 2 + j)
            for i in (0, 1):
                pb[h, j * 2 + i, 0] = o[i * 128 : (i + 1) * 128]
                pb[h, j * 2 + i, 1] = do[i * 128 : (i + 1) * 128]
            return 0

        def for_self(j, _):
            o, do = attend(h, y * 2 + j)
            for i in (0, 1):
                ob[j * 2 + i, y, 0, :, own_col] = o[i * 128 : (i + 1) * 128]
                ob[j * 2 + i, y, 1, :, own_col] = do[i * 128 : (i + 1) * 128]
            return 0

        if h < 2:
            lax.fori_loop(0, 2, for_partner, 0)
            swap(h, 0)
        else:
            for_partner(0, 0)
            for earlier, pair in ((2, 0), (0, 1), (1, 1)):
                swap(earlier, pair)
            for_partner(1, 0)
            swap(2, 1)
        lax.fori_loop(0, 2, for_self, 0)

    def unit(p, part, which, from_x):
        rb, first, rows = PIECES[p]
        skip, width = PARTS[part]
        col = pl.ds(pl.multiple_of(from_x * GW + skip, 128), width)
        group = y if which == 0 else 1 - y
        k = p * 4 + part * 2 + which if p < 2 else 4 + p * 2 + which
        return ob.at[rb, group, :, pl.ds(first, rows), col], k

    def x_unit(p, part, which):
        src, k = unit(p, part, which, x)
        send(src, src, x_send, x_recv.at[k], right)
        send(src, src, x_send, x_recv.at[k], left)

    def forward(p, part, which):
        rb, first, rows = PIECES[p]
        src, k = unit(p, part, which, xl)
        two = ob.at[rb, :, :, pl.ds(first, rows), pl.ds(0, PARTS[part][1])]
        wait(two, x_recv.at[k])
        send(src.at[0], src.at[0], x_send, f_recv.at[p], right)
        src, k = unit(p, part, which, xr)
        send(src.at[1], src.at[1], x_send, f_recv.at[p], left)

    def all_unit(p, which):
        x_unit(p, 2, which)
        src, _ = unit(p, 2, which, x)
        send(src, src, x_send, f_recv.at[p], {"dp": dp, "head": y * X + lax.rem(x + 2, X)})

    def arrived(p):
        rb, first, rows = PIECES[p]
        wait(ob.at[rb, :, :, pl.ds(first, rows), pl.ds(0, GW)], f_recv.at[p])

    def arrived_near(p):
        rb, first, rows = PIECES[p]
        for which in (0, 1):
            _, k = unit(p, 2, which, x)
            wait(ob.at[rb, :, :, pl.ds(first, rows), pl.ds(0, GW)], x_recv.at[k])

    wait(shard(3).at[z, c], wy_recv.at[3])
    shard_along_z(3)

    wait(recv.at[0, 2], v_recv.at[0])
    wait(recv.at[1, 2], v_recv.at[1])
    sends_q(1)
    sends_v(2)

    shard_to_core(0)
    wait(gall.at[:, z, c], g_recv.at[0])
    for d in (1, 3, 2):
        send(gall.at[:, z, c], gall.at[:, z, c], g_send.at[1], g_recv.at[1], z_peer(d))

    wait(recv.at[0, pl.ds(0, 2)], q_recv.at[0])
    sends_q(2)
    src = shard(0).at[z, c]
    send(src, src, wy_send, wy_recv.at[1], y_chip(1))
    attention(0)

    shard_to_core(3)
    wait(recv.at[1, pl.ds(0, 2)], q_recv.at[1])
    attention(1)
    x_unit(0, 0, 0)
    x_unit(1, 0, 0)

    wait(gall.at[:, pl.ds(0, 3), c], g_recv.at[1])
    send(gall.at[:, :, c], gall.at[:, :, c], g_send.at[2], g_recv.at[2], other_core)

    wait(recv.at[2], q_recv.at[2])
    attention(2)
    x_unit(0, 1, 0)
    x_unit(1, 1, 0)
    wait(shard(1).at[z, c], wy_recv.at[1])
    shard_along_z(1)
    src = shard(1).at[z, c]
    send(src, src, wy_send, wy_recv.at[2], y_chip(3))
    forward(0, 0, 0)
    forward(1, 0, 0)
    x_unit(2, 2, 0)
    swapped(0)
    x_unit(0, 0, 1)
    wait(shard(2).at[z, c], wy_recv.at[2])
    shard_along_z(2)
    forward(0, 1, 0)
    swapped(1)
    x_unit(0, 1, 1)
    x_unit(1, 0, 1)
    forward(0, 0, 1)
    shard_to_core(1)
    forward(1, 1, 0)
    x_unit(1, 1, 1)
    forward(0, 1, 1)
    forward(1, 0, 1)
    forward(1, 1, 1)
    swapped(2)
    x_unit(2, 2, 1)
    x_unit(3, 2, 0)

    wait(gall.at[:, :, 1 - c], g_recv.at[2])
    moment = time[dp].astype(F32)
    speed = ttan[dp]
    freq = const[1:2, :]
    cos_t, sin_t = jnp.cos(moment * freq), jnp.sin(moment * freq)
    row = lax.broadcasted_iota(jnp.int32, (16, 256), 0)
    emb = jnp.concatenate([cos_t, sin_t], axis=1)
    demb = jnp.concatenate([-freq * sin_t, freq * cos_t], axis=1) * speed
    embs = jnp.where(row == 0, emb, jnp.where(row == 1, demb, 0.0)).astype(BF)
    gates = jnp.dot(embs, gall[...].reshape(256, COLS), preferred_element_type=F32)
    gate, dgate = gates[0:1], gates[1:2]

    wait(wall.at[1 - y, :, :, 1 - c], wc_recv.at[1])
    wait(resv, res_sem)

    def finish(rows, attn, dattn):
        out[rows, :] = (resv[0, rows, :].astype(F32) + gate * attn).astype(BF)
        otan[rows, :] = (resv[1, rows, :].astype(F32) + dgate * attn + gate * dattn).astype(BF)

    def project(rb, first, rows, yl):
        total = None
        for gy in (0, 1):
            term = jnp.dot(
                ob[rb, gy, :, first : first + rows, :].reshape(2 * rows, 1536),
                wall[yl, gy].reshape(1536, COLS),
                preferred_element_type=F32,
            )
            total = term if total is None else total + term
        return total

    def project_from(rb, first, rows, yl, offsets):
        total = None
        for gy in (0, 1):
            for offset in offsets:
                at = lax.rem(x + offset, X)
                col = pl.ds(pl.multiple_of(at * GW, 128), GW)
                term = jnp.dot(
                    ob[rb, gy, :, first : first + rows, col].reshape(2 * rows, GW),
                    wall[yl, gy, at].reshape(GW, COLS),
                    preferred_element_type=F32,
                )
                total = term if total is None else total + term
        return total

    def own_block(rb):
        total = project(rb, 0, ROWS, y)
        start = pl.multiple_of(y * HALF + rb * ROWS, ROWS)
        finish(pl.ds(start, ROWS), total[:ROWS], total[ROWS:])

    for p, (rb, first, rows) in enumerate(PIECES):
        if p == ALL:
            arrived_near(p)
            near = project_from(rb, first, 2 * rows, 1 - y, (0, 1, 3))
        arrived(p)
        if p < ALL:
            total = project(rb, first, rows, 1 - y)
        else:
            at = (p - ALL) * rows
            total = jnp.concatenate([near[at : at + rows], near[2 * rows + at : 3 * rows + at]])
            total = total + project_from(rb, first, rows, 1 - y, (2,))
        both = pl.ds(0, 2 * rows)
        po[p, both] = total.astype(BF)
        send(po.at[p, both], pr.at[p, both], y_send, y_recv.at[p], partner)
        if p == 0:
            forward(2, 2, 0)
            x_unit(3, 2, 1)
            shard_to_core(2)
        elif p == 1:
            forward(2, 2, 1)
            x_unit(4, 2, 0)
            forward(3, 2, 0)
            x_unit(4, 2, 1)
            wait(wall.at[y, :, :, 1 - c], wc_recv.at[0])
            own_block(0)
        elif p == 2:
            forward(3, 2, 1)
            x_unit(6, 2, 0)
            forward(4, 2, 0)
            x_unit(6, 2, 1)
            forward(4, 2, 1)
            all_unit(ALL, 0)
            all_unit(ALL, 1)
            own_block(1)
        elif p == 3:
            own_block(2)
            forward(6, 2, 0)
            forward(6, 2, 1)
        elif p == 6:
            own_block(3)

    wait(sv.at[:, pl.ds(0, 7)], v_send)
    wait(sq.at[:, pl.ds(0, 7)], q_send)
    wait(pb, pre_send)
    wait(wall.at[0, 0, pl.ds(0, 3), 0], wy_send)
    wait(wall.at[:, :, pl.ds(0, 3), 0], wz_send)
    wait(wall.at[:, :, :, 0], wc_send)
    wait(gall.at[0, 0, 0], g_send.at[0])
    wait(gall.at[:, pl.ds(0, 3), 0], g_send.at[1])
    wait(gall.at[:, :, 0], g_send.at[2])
    wait(ob.at[:, :, :, :, pl.ds(0, 3 * GW)], x_send)

    for p, (rb, first, rows) in enumerate(PIECES):
        wait(pr.at[p, pl.ds(0, 2 * rows)], y_recv.at[p])
        start = pl.multiple_of((1 - y) * HALF + rb * 128 + first, 32)
        finish(
            pl.ds(start, rows),
            pr[p, 0:rows].astype(F32),
            pr[p, rows : 2 * rows].astype(F32),
        )
    wait(po.at[pl.ds(0, 4)], y_send)


def copy_kernel(a, b, out_a, out_b, sem):
    copies = (
        pltpu.make_async_copy(a, out_a, sem.at[0]),
        pltpu.make_async_copy(b, out_b, sem.at[1]),
    )
    for copy in copies:
        copy.start()
    for copy in copies:
        copy.wait()


def per_device(
    projections,
    projection_tangent,
    position_ids,
    norm_gain,
    out_weight,
    timestep,
    time_tangent,
    gate_weight,
    residual,
    residual_tangent,
):
    anywhere = pl.BlockSpec(memory_space=pl.ANY)
    dma = pltpu.SemaphoreType.DMA
    shape = jax.ShapeDtypeStruct((SEQ, COLS), BF)
    results = pl.pallas_call(
        kernel,
        out_shape=(pltpu.VMEM((SEQ, COLS), BF),) * 2,
        in_specs=[pl.BlockSpec(memory_space=pltpu.HBM)] * 11,
        out_specs=(pl.BlockSpec(memory_space=pltpu.VMEM),) * 2,
        scratch_shapes=[
            pltpu.VMEM((3, ROWS), jnp.int32),
            pltpu.VMEM((2, ATT_W), F32),
            pltpu.SMEM((16,), jnp.int32),
            pltpu.SMEM((16,), F32),
            pltpu.VMEM((8, 128), F32),
            pltpu.VMEM((2, 2, ROWS, ATT_W), BF),
            pltpu.VMEM((3, 8, ROWS, 256), BF),
            pltpu.VMEM((3, 8, 2, ROWS, 256), BF),
            pltpu.VMEM((3, 3, SEQ, 256), BF),
            pltpu.VMEM((4, 2, 2, ROWS, 1536), BF),
            pltpu.VMEM((3, 4, 2, ROWS, 128), BF),
            pltpu.VMEM((2, 2, 4, 2, 192, COLS), BF),
            pltpu.VMEM((2, 4, 2, 16, COLS), BF),
            pltpu.VMEM((2, SEQ, COLS), BF),
            pltpu.VMEM((7, 256, COLS), BF),
            pltpu.VMEM((7, 256, COLS), BF),
            dma((5,)),
            dma((2,)),
            dma,
            dma,
            dma((2,)),
            dma,
            dma((3,)),
            dma,
            dma((3,)),
            dma,
            dma((4,)),
            dma,
            dma((4,)),
            dma,
            dma((2,)),
            dma((3,)),
            dma((3,)),
            dma,
            dma((18,)),
            dma((7,)),
            dma,
            dma((7,)),
        ],
        compiler_params=pltpu.CompilerParams(
            collective_id=0, has_side_effects=True, vmem_limit_bytes=56 * 2**20
        ),
    )(
        projections,
        projection_tangent,
        position_ids.T,
        norm_gain,
        out_weight,
        timestep,
        time_tangent,
        gate_weight,
        residual,
        residual_tangent,
        jnp.asarray(CONST),
    )
    return pl.pallas_call(
        copy_kernel,
        out_shape=(shape, shape),
        in_specs=[anywhere, anywhere],
        out_specs=(anywhere, anywhere),
        scratch_shapes=[dma((2,))],
        compiler_params=pltpu.CompilerParams(vmem_limit_bytes=8 * 2**20),
    )(*results)


def solution(mesh):
    placed = (
        P(None, ("dp", "head"), None),
        P(None, ("dp", "head"), None),
        P(("dp", "head"), None),
        P(),
        P("dp", "head"),
        P(),
        P(),
        P("dp", None),
        P("dp", "head"),
        P("dp", "head"),
    )
    return jax.shard_map(
        per_device,
        mesh=mesh,
        in_specs=placed,
        out_specs=(P("dp", "head"), P("dp", "head")),
        check_vma=False,
    )
```
